128 devices in a mesh: tm: 32 (over x, z, y_hi), head: 4 (over y_lo, core).
Axes of the slice: x: 4, y: 4 (y_hi: 2, y_lo: 2; y = y_hi * 2 + y_lo), z: 4, core: 2. Of those that a mesh axis runs over, the one named last changes fastest.
Arguments:
- queries: bfloat16 [12288, 2560], P(('tm', 'head')), may hold values from -8 to 8
- keys: bfloat16 [12288, 2560], P(('tm', 'head')), may hold values from -8 to 8
- values: bfloat16 [12288, 2560], P(('tm', 'head')), may hold values from -6 to 6
- w_out: bfloat16 [2560, 5120], P('head'), may hold values from -0.125 to 0.125
- block_mask: int32 [192, 192], replicated, may hold values from 0 to 1, as said below
- frame_map: int32 [32], replicated, may hold values from 0 to 31, each once
Outputs:
- projected: bfloat16 [12288, 5120], P(('tm', 'head'))
The draws below stay inside these ranges and needn't reach their ends.
Inputs may be any that keep to these rules, and one draw needn't show every extreme that they name: block_mask is 1 where a query block may read a key block; all blocks of a frame may read all blocks of the same frame, and every query block may read the block of the same place in every frame. frame_map is a permutation of the frames.
All inputs are finite; a program needn't handle non-finite values.
Results may differ from the reference program's by a relative error of at most 0.019.
Values may be sent and summed in bfloat16 or wider, within the bound.
No kernel may reach another device: no remote copies, remote signals or barrier semaphores. Data moves between devices by JAX's collectives and lax.ppermute only.
A program may use at most 192 MiB of HBM per device.

```python
import jax
import jax.numpy as jnp
from jax import lax

D = 5120
HEADS = 20
HS = 128
BLOCK = 64
FRAME = 384
FRAMES = 32
TOKENS = 12288
FB = 6
NBLK = 192
HH = 2560
N_HEAD = 4


def draw_queries(key, part):
    key = jax.random.fold_in(key, 1)
    normal_part = jax.random.normal(key, (TOKENS, HH), jnp.float32)
    normal_part = jnp.clip(normal_part, -8.0, 8.0)
    return normal_part.astype(jnp.bfloat16)


def draw_keys(key, part):
    key = jax.random.fold_in(key, 2)
    normal_part = jax.random.normal(key, (TOKENS, HH), jnp.float32)
    normal_part = jnp.clip(normal_part, -8.0, 8.0)
    return normal_part.astype(jnp.bfloat16)


def draw_block_mask(key, part):
    key = jax.random.fold_in(key, 7)
    block_ids = jnp.arange(NBLK, dtype=jnp.int32)
    frame_ids = block_ids // FB
    place_ids = block_ids % FB
    distance = jnp.abs(frame_ids[:, None] - frame_ids[None, :])
    level = jnp.zeros((NBLK, NBLK), jnp.int32)
    for power in range(1, 12):
        level = level + (distance >= 2 ** power).astype(jnp.int32)
    band_width = jnp.right_shift(jnp.int32(FB), level)
    offset = jnp.abs(place_ids[:, None] - place_ids[None, :])
    banded = offset <= band_width
    sprinkled = jax.random.randint(key, (NBLK, NBLK), 0, 8) == 0
    kept = (distance == 0) | banded | sprinkled
    return kept.astype(jnp.int32)


def block_scale(own_key, extent, split, least, top_value):
    def one(dim, shards_of):
        heights = jax.random.uniform(jax.random.fold_in(jax.random.fold_in(own_key, 6), dim), (shards_of,), jnp.float32, least / len(split), top_value / len(split))
        return jnp.repeat(jnp.exp(heights), extent[dim] // shards_of).reshape((-1,) + (1,) * (len(extent) - dim - 1))

    gain = one(*split[0])
    for cut in split[1:]:
        gain = gain * one(*cut)
    return gain


def noise(key, shape, spread, most, split=(), held_as=jnp.bfloat16):
    loudness = block_scale(key, shape, split, -0.22, 0.18) if split else 1.0
    values = jax.random.normal(key, shape, jnp.float32) * spread * loudness
    return jnp.minimum(jnp.maximum(values, -most), most).astype(held_as)


def setup_inputs(seed: int = 0) -> dict:
    arg_keys = jax.random.split(jax.random.key(seed), 7)
    queries = draw_queries(jax.random.fold_in(arg_keys[6], 71), 0)
    keys = draw_keys(jax.random.fold_in(arg_keys[6], 71), 0)
    values = noise(arg_keys[2], (TOKENS, HH), 1.0, 6.0, ((0, 128),))
    w_out = noise(arg_keys[3], (HH, D), HH ** -0.5, 0.125, ((0, 4),))
    block_mask = draw_block_mask(jax.random.fold_in(arg_keys[6], 71), 0)
    frame_map = jax.random.permutation(arg_keys[5], FRAMES).astype(jnp.int32)
    return {"queries": queries, "keys": keys, "values": values, "w_out": w_out, "block_mask": block_mask, "frame_map": frame_map}


NEG = -1.0e30


def reference(queries, keys, values, w_out, block_mask, frame_map):
    frame_blocks = FRAME // BLOCK
    block_order = (frame_map[:, None] * frame_blocks + jnp.arange(frame_blocks, dtype=jnp.int32)[None, :]).reshape(-1).astype(jnp.int32)
    placed = block_mask[block_order][:, block_order]
    keys_all = keys.astype(jnp.float32).reshape(TOKENS, HEADS, HS)
    values_all = values.astype(jnp.float32).reshape(TOKENS, HEADS, HS)
    group_width = HEADS // N_HEAD * HS

    def one_frame(frame_index):
        query_rows = lax.dynamic_slice_in_dim(queries, frame_index * FRAME, FRAME, 0).astype(jnp.float32).reshape(FRAME, HEADS, HS)
        mask_rows = lax.dynamic_slice_in_dim(placed, frame_index * frame_blocks, frame_blocks, 0)
        allowed = jnp.broadcast_to(mask_rows[:, None, :, None] > 0, (frame_blocks, BLOCK, NBLK, BLOCK)).reshape(FRAME, TOKENS)
        scores = jnp.einsum("qhd,khd->hqk", query_rows, keys_all) * (HS ** -0.5)
        scores = jnp.where(allowed[None], scores, NEG)
        running_max = jnp.max(scores, axis=-1, keepdims=True)
        weights = jnp.where(allowed[None], jnp.exp(scores - running_max), 0.0)
        row_sum = jnp.sum(weights, axis=-1)
        rounded = lax.optimization_barrier(weights.astype(jnp.bfloat16)).astype(jnp.float32)
        mixed_heads = jnp.einsum("hqk,khd->qhd", rounded, values_all) / jnp.transpose(row_sum)[:, :, None]
        attended = mixed_heads.reshape(FRAME, HEADS * HS).astype(jnp.bfloat16)
        summed = jnp.zeros((FRAME, D), jnp.float32)
        for group in range(N_HEAD):
            term = jnp.dot(attended[:, group * group_width:(group + 1) * group_width], w_out[group * group_width:(group + 1) * group_width], preferred_element_type=jnp.float32)
            summed = summed + lax.optimization_barrier(term.astype(jnp.bfloat16)).astype(jnp.float32)
        return summed.astype(jnp.bfloat16)

    result = lax.map(one_frame, jnp.arange(FRAMES, dtype=jnp.int32))
    return result.reshape(TOKENS, D)
```

```python
import functools

import jax
import jax.numpy as jnp
import numpy as np
from jax import lax
from jax.experimental import pallas as pl
from jax.experimental.pallas import tpu as pltpu
from jax.sharding import PartitionSpec as P

HS = 128
BLOCK = 64
FRAME = 384
FB = FRAME // BLOCK
SUB = 32
NEG = -1e30
SCALE = HS ** -0.5
LOG2 = float(SCALE * np.log2(np.e))
BOUND = 60.0

RING = ("z", "yh", "yl")
Y = ("yh", "yl")
ALL = ("x", "z", "yh", "yl", "c")
ROWS = 144


def square_norm_max(rows):
    wide = rows.astype(jnp.float32)
    return jnp.max(jnp.sum(wide * wide, axis=1, keepdims=True))


def attention_kernel(*refs, first, column, step):
    if first:
        q_ref, k_ref, vt_ref, mt_ref, state_out, flag_out = refs
    else:
        flag_in, q_ref, k_ref, vt_ref, mt_ref, state_in, state_out, flag_out = refs
    tile = pl.program_id(0)
    rows = q_ref.shape[0]
    keys = k_ref.shape[0]
    bounded = square_norm_max(q_ref[...]) * square_norm_max(k_ref[...]) <= (BOUND / SCALE) ** 2
    if not first:
        bounded = jnp.logical_and(bounded, flag_in[tile] == 1)
    place = lax.broadcasted_iota(jnp.int32, (rows, HS), 0) // SUB + (column + tile * (rows // SUB))
    one_hot = jnp.where(place == lax.broadcasted_iota(jnp.int32, (rows, HS), 1), 1.0, 0.0).astype(jnp.bfloat16)
    query = jnp.concatenate([q_ref[...], one_hot], axis=1)

    def scores(at):
        masks = mt_ref[at // SUB : (at + step) // SUB, :]
        masks = jnp.broadcast_to(masks[:, None, :], (step // SUB, SUB, HS)).reshape(step, HS)
        key = jnp.concatenate([k_ref[at : at + step, :], masks.astype(jnp.bfloat16)], axis=1)
        return lax.dot_general(key, query, (((1,), (1,)), ((), ())), preferred_element_type=jnp.float32)

    @pl.when(bounded)
    def _():
        if first:
            weighted = jnp.zeros((HS, rows), jnp.float32)
            total = jnp.zeros((1, rows), jnp.float32)
        else:
            weighted = state_in[0, :HS, :]
            total = state_in[0, HS : HS + 1, :]
        for at in range(0, keys, step):
            weights = jnp.exp2(scores(at) * LOG2)
            total = total + jnp.sum(weights, axis=0, keepdims=True)
            weighted = weighted + jnp.dot(
                vt_ref[:, at : at + step], weights.astype(jnp.bfloat16), preferred_element_type=jnp.float32
            )
        state_out[0, :HS, :] = weighted
        state_out[0, HS : HS + 8, :] = jnp.broadcast_to(total, (8, rows))
        state_out[0, HS + 8 :, :] = jnp.zeros((8, rows), jnp.float32)
        flag_out[tile] = 1

    @pl.when(jnp.logical_not(bounded))
    def _():
        if first:
            weighted = jnp.zeros((HS, rows), jnp.float32)
            total = jnp.zeros((1, rows), jnp.float32)
            top = jnp.full((1, rows), NEG, jnp.float32)
        else:
            weighted = state_in[0, :HS, :]
            total = state_in[0, HS : HS + 1, :]
            top = state_in[0, HS + 8 : HS + 9, :]
        for at in range(0, keys, step):
            found = scores(at)
            new_top = jnp.maximum(top, jnp.max(found, axis=0, keepdims=True))
            factor = jnp.exp2((top - new_top) * LOG2)
            weights = jnp.exp2((found - new_top) * LOG2)
            total = total * factor + jnp.sum(weights, axis=0, keepdims=True)
            weighted = weighted * factor + jnp.dot(
                vt_ref[:, at : at + step], weights.astype(jnp.bfloat16), preferred_element_type=jnp.float32
            )
            top = new_top
        state_out[0, :HS, :] = weighted
        state_out[0, HS : HS + 8, :] = jnp.broadcast_to(total, (8, rows))
        state_out[0, HS + 8 :, :] = jnp.broadcast_to(top, (8, rows))
        flag_out[tile] = 0


def attention(query, key, value_t, masks, column, state=None, step=512):
    tiles, rows, _ = query.shape
    keys = key.shape[0]
    first = state is None
    smem = pl.BlockSpec(memory_space=pltpu.SMEM)
    state_spec = pl.BlockSpec((1, ROWS, rows), lambda i: (i, 0, 0))
    specs = [
        pl.BlockSpec((None, rows, HS), lambda i: (i, 0, 0)),
        pl.BlockSpec((keys, HS), lambda i: (0, 0)),
        pl.BlockSpec((HS, keys), lambda i: (0, 0)),
        pl.BlockSpec((keys // SUB, HS), lambda i: (0, 0)),
    ]
    operands = [query, key, value_t, masks]
    if not first:
        specs = [smem] + specs + [state_spec]
        operands = [state[1]] + operands + [state[0]]
    count = tiles * rows * keys
    return pl.pallas_call(
        functools.partial(attention_kernel, first=first, column=column, step=min(step, keys)),
        grid=(tiles,),
        in_specs=specs,
        out_specs=[state_spec, smem],
        out_shape=[
            jax.ShapeDtypeStruct((tiles, ROWS, rows), jnp.float32),
            jax.ShapeDtypeStruct((tiles,), jnp.int32),
        ],
        input_output_aliases={} if first else {5: 0},
        cost_estimate=pl.CostEstimate(flops=count * 1024, bytes_accessed=tiles * ROWS * rows * 8, transcendentals=count),
        compiler_params=pltpu.CompilerParams(vmem_limit_bytes=40 * 2**20),
    )(*operands)


def merge_kernel(own_ref, other_ref, out_ref):
    own_top = own_ref[HS + 8 : HS + 9, :]
    other_top = other_ref[HS + 8 : HS + 9, :]
    top = jnp.maximum(own_top, other_top)
    own_factor = jnp.exp2((own_top - top) * LOG2)
    other_factor = jnp.exp2((other_top - top) * LOG2)
    total = own_ref[HS : HS + 1, :] * own_factor + other_ref[HS : HS + 1, :] * other_factor
    mixed = own_ref[:HS, :] * own_factor + other_ref[:HS, :] * other_factor
    out_ref[...] = jnp.transpose(mixed / total).astype(jnp.bfloat16)


def merge(own, other):
    rows = own.shape[1]
    return pl.pallas_call(
        merge_kernel,
        out_shape=jax.ShapeDtypeStruct((rows, HS), jnp.bfloat16),
        compiler_params=pltpu.CompilerParams(vmem_limit_bytes=32 * 2**20),
    )(own, other)


def project_kernel(rank_ref, att_ref, w0, w1, w2a, w2b, w3a, w3b, out_ref):
    rank = rank_ref[0]

    def group(number):
        return jnp.concatenate([att_ref[number * 5 + i] for i in range(5)], axis=1)

    def product(rows, weight):
        return jnp.dot(rows, weight[...], preferred_element_type=jnp.float32)

    own, side = group(rank), group(rank ^ 1)
    far, far_side = group(rank ^ 2), group(rank ^ 3)
    half = w2a.shape[0]
    total = product(own, w0) + product(side, w1)
    total = total + product(far[:, :half], w2a) + product(far[:, half:], w2b)
    total = total + product(far_side[:, :half], w3a) + product(far_side[:, half:], w3b)
    out_ref[...] = total.astype(jnp.bfloat16)


def project(rank, attended, weights, width=512):
    heads, rows, _ = attended.shape
    columns = weights[0].shape[1]
    return pl.pallas_call(
        project_kernel,
        grid=(columns // width,),
        in_specs=[pl.BlockSpec(memory_space=pltpu.SMEM), pl.BlockSpec((heads, rows, HS), lambda j: (0, 0, 0))]
        + [pl.BlockSpec((w.shape[0], width), lambda j: (0, j)) for w in weights],
        out_specs=pl.BlockSpec((rows, width), lambda j: (0, j)),
        out_shape=jax.ShapeDtypeStruct((rows, columns), jnp.bfloat16),
        cost_estimate=pl.CostEstimate(
            flops=2 * rows * heads * HS * columns, bytes_accessed=heads * HS * columns * 2, transcendentals=0
        ),
        compiler_params=pltpu.CompilerParams(vmem_limit_bytes=40 * 2**20),
    )(rank, attended, *weights)


def ring(array, axes, size, shift):
    return lax.ppermute(array, axes, [(i, (i + shift) % size) for i in range(size)])


def swap(array):
    return lax.ppermute(array, "c", [(0, 1), (1, 0)])


def mask_table(block_mask, frame_map, key_x):
    x, z, core = lax.axis_index("x"), lax.axis_index("z"), lax.axis_index("c")
    rows = len(key_x) * 48
    row = jnp.arange(rows, dtype=jnp.int32)
    column = jnp.arange(HS, dtype=jnp.int32)
    row_x = jnp.stack(key_x)[row // 48]

    def block_of(at_x, at_z, inner, at_core):
        frame = (at_x * 4 + at_z) * 2 + inner // 6
        within = ((((inner // 3) % 2) * 2 + at_core) * 96 + (inner % 3) * SUB) // BLOCK
        stored = jnp.sum(jnp.where(frame[:, None] == jnp.arange(32, dtype=jnp.int32)[None, :], frame_map[None, :], 0), axis=1)
        return stored * FB + within

    key_block = block_of(row_x, (row % 48) // 12, row % 12, core)
    ring_part = column < 96
    local = jnp.where(ring_part, column % 48, (column - 96) % 12)
    other = jnp.where(ring_part, column // 48, (column - 96) // 12)
    query_block = block_of(x, jnp.where(ring_part, local // 12, z), local % 12, core ^ (other & 1))
    blocks = jnp.arange(block_mask.shape[0], dtype=jnp.int32)
    key_pick = (key_block[:, None] == blocks[None, :]).astype(jnp.bfloat16)
    query_pick = (query_block[:, None] == blocks[None, :]).astype(jnp.bfloat16)
    blocked = (block_mask <= 0).astype(jnp.bfloat16)
    by_query = jnp.dot(query_pick, blocked, preferred_element_type=jnp.float32).astype(jnp.bfloat16)
    return lax.dot_general(key_pick, by_query, (((1,), (1,)), ((), ())), preferred_element_type=jnp.float32) * NEG


def local(queries, keys, values, w_out, block_mask, frame_map):
    x = lax.axis_index("x")
    rank = (lax.axis_index("yl") * 2 + lax.axis_index("c")).astype(jnp.int32)
    token_rows = queries.shape[0]
    parts = jnp.stack([queries, keys, values]).reshape(3, token_rows, 20, HS).transpose(2, 0, 1, 3)
    ring_part = lax.all_to_all(parts[:16], RING, 0, 0)
    plane_part = lax.all_to_all(parts[16:], Y, 0, 0)
    qa, ka, va = (ring_part[:, i].reshape(-1, HS) for i in range(3))
    qb, kb, vb = (plane_part[:, i].reshape(-1, HS) for i in range(3))

    masks = mask_table(block_mask, frame_map, [x, (x + 3) % 4, (x + 1) % 4, (x + 2) % 4])

    plane_all = lax.all_gather(jnp.concatenate([kb, vb], axis=0), ("x", "z"), axis=0, tiled=True)
    plane_all = plane_all.reshape(4, 4, 2, kb.shape[0], HS)

    both = swap(jnp.concatenate([qa, qb], axis=0))
    query_a = jnp.stack([qa, both[: qa.shape[0]]])
    query_b = jnp.concatenate([qb, both[qa.shape[0] :]], axis=0)[None]
    vta = jnp.transpose(va)
    k_left, k_right = ring(ka, "x", 4, 1), ring(ka, "x", 4, -1)
    v_left, v_right = ring(vta, "x", 4, 1), ring(vta, "x", 4, -1)
    half = ka.shape[0] // 2
    k_far = jnp.concatenate([ring(k_left[:half], "x", 4, 1), ring(k_right[half:], "x", 4, -1)], axis=0)
    v_far = jnp.concatenate([ring(v_left[:, :half], "x", 4, 1), ring(v_right[:, half:], "x", 4, -1)], axis=1)

    w_side = swap(w_out)
    middle = w_out.shape[0] // 2
    w_far = [ring(w_out[:middle], Y, 4, 1), ring(w_out[middle:], Y, 4, -1)]
    w_far_side = [swap(w_far[0]), swap(w_far[1])]

    state = attention(query_a, ka, vta, masks[:48], 0)
    state = attention(query_a, k_left, v_left, masks[48:96], 0, state)
    state = attention(query_a, k_right, v_right, masks[96:144], 0, state)
    state = attention(query_a, k_far, v_far, masks[144:], 0, state)

    plane_keys = plane_all[:, :, 0].reshape(4, -1, HS)
    plane_values = plane_all[:, :, 1].reshape(4, -1, HS)
    order = [x, (x + 3) % 4, (x + 1) % 4, (x + 2) % 4]
    plane_masks = lax.dynamic_update_slice_in_dim(jnp.zeros_like(masks), masks[:48], x * 48, 0)
    for i in range(1, 4):
        plane_masks = lax.dynamic_update_slice_in_dim(plane_masks, masks[48 * i : 48 * (i + 1)], order[i] * 48, 0)
    plane_state = attention(
        query_b, plane_keys.reshape(-1, HS), jnp.transpose(plane_values.reshape(-1, HS)), plane_masks, 96
    )

    plane_rows = qb.shape[0]
    other_a = swap(state[0][1])
    other_b = swap(plane_state[0][0][:, plane_rows:])
    out_a = merge(state[0][0], other_a)
    out_b = merge(plane_state[0][0][:, :plane_rows], other_b)
    back_a = lax.all_to_all(out_a.reshape(16, token_rows, HS), RING, 0, 0)
    back_b = lax.all_to_all(out_b.reshape(4, token_rows, HS), Y, 0, 0)
    attended = jnp.concatenate([back_a, back_b], axis=0)
    return project(rank[None], attended, [w_out, w_side] + w_far + w_far_side)


def solution(mesh):
    fine = jax.sharding.Mesh(mesh.devices.reshape(4, 4, 2, 2, 2), ALL)
    rows = P(ALL, None)
    placed = (rows, rows, rows, P(("yl", "c"), None), P(), P())
    return jax.shard_map(local, mesh=fine, in_specs=placed, out_specs=rows, check_vma=False)
```

```python
import functools

import jax
import jax.numpy as jnp
import numpy as np
from jax import lax
from jax.experimental import pallas as pl
from jax.experimental.pallas import tpu as pltpu
from jax.sharding import PartitionSpec as P

HS = 128
BLOCK = 64
FRAME = 384
FB = FRAME // BLOCK
NEG = -1e30
SCALE = HS ** -0.5
LOG2 = float(SCALE * np.log2(np.e))
BOUND = 60.0

RING = ("z", "yh", "yl")
Y = ("yh", "yl")
ALL = ("x", "z", "yh", "yl", "c")
PROJECT_VMEM = 20
CHUNKS = 2
NEAR = (0, 3, 1, 2)
ROWS = 144


def square_norm_max(rows):
    wide = rows.astype(jnp.float32)
    return jnp.max(jnp.sum(wide * wide, axis=1, keepdims=True))


def attention_kernel(*refs, first, count, parts, sub, small):
    q_ref, mt_ref = refs[0], refs[1]
    sources = refs[2 : 2 + count]
    if first:
        state_in = norm_in = None
        state_out, norm_out = refs[2 + count :]
    else:
        norm_in, state_in, state_out, norm_out = refs[2 + count :]
    tiles, rows, _ = q_ref.shape

    def joined(slices):
        return slices[0] if len(slices) == 1 else jnp.concatenate(slices, axis=0)

    def with_masks(key, tile, mask_at, size):
        masks = mt_ref[tile, pl.ds(mask_at, size // sub), :]
        masks = jnp.broadcast_to(masks[:, None, :], (size // sub, sub, HS)).reshape(size, HS)
        return jnp.concatenate([key, masks.astype(jnp.bfloat16)], axis=1)

    def scores(key, query):
        return lax.dot_general(key, query, (((1,), (1,)), ((), ())), preferred_element_type=jnp.float32)

    def mixed(value, weights):
        return lax.dot_general(
            value, weights.astype(jnp.bfloat16), (((0,), (0,)), ((), ())), preferred_element_type=jnp.float32
        )

    key_norm = jnp.float32(0.0)
    for k_source, k_at, _, _, keys in parts:
        key_norm = jnp.maximum(key_norm, square_norm_max(sources[k_source][k_at : k_at + keys, :]))
    all_keys = sum(part[4] for part in parts)

    @pl.loop(0, tiles)
    def _(tile):
        query_norm = square_norm_max(q_ref[tile]) if first else jnp.max(norm_in[tile])
        bounded = jnp.logical_and(query_norm >= 0.0, query_norm * key_norm <= (BOUND / SCALE) ** 2)
        place = lax.broadcasted_iota(jnp.int32, (rows, HS), 0) // sub
        one_hot = jnp.where(place == lax.broadcasted_iota(jnp.int32, (rows, HS), 1), 1.0, 0.0).astype(jnp.bfloat16)
        query = jnp.concatenate([q_ref[tile], one_hot], axis=1)
        norm_out[tile] = jnp.full((8, HS), jnp.where(bounded, query_norm, -1.0), jnp.float32)

        @pl.when(bounded)
        def _():
            key = joined([sources[k][at : at + keys, :] for k, at, _, _, keys in parts])
            value = joined([sources[v][at : at + keys, :] for _, _, v, at, keys in parts])
            weights = jnp.exp2(scores(with_masks(key, tile, 0, all_keys), query) * LOG2)
            total = jnp.sum(weights, axis=0, keepdims=True)
            weighted = mixed(value, weights)
            if not first:
                total = state_in[tile, HS : HS + 1, :] + total
                weighted = state_in[tile, :HS, :] + weighted
            state_out[tile, :HS, :] = weighted
            state_out[tile, HS : HS + 8, :] = jnp.broadcast_to(total, (8, rows))
            state_out[tile, HS + 8 :, :] = jnp.zeros((8, rows), jnp.float32)

        @pl.when(jnp.logical_not(bounded))
        def _():
            if first:
                state_out[tile, : HS + 8, :] = jnp.zeros((HS + 8, rows), jnp.float32)
                state_out[tile, HS + 8 :, :] = jnp.full((8, rows), NEG, jnp.float32)
            else:
                state_out[tile] = state_in[tile]
            mask_base = 0
            for k_source, k_at, v_source, v_at, keys in parts:

                @pl.loop(0, keys // small)
                def _(j):
                    key = sources[k_source][pl.ds(pl.multiple_of(k_at + j * small, small), small), :]
                    value = sources[v_source][pl.ds(pl.multiple_of(v_at + j * small, small), small), :]
                    mask_at = pl.multiple_of(mask_base + j * (small // sub), 8)
                    found = scores(with_masks(key, tile, mask_at, small), query)
                    top = state_out[tile, HS + 8 : HS + 9, :]
                    new_top = jnp.maximum(top, jnp.max(found, axis=0, keepdims=True))
                    factor = jnp.exp2((top - new_top) * LOG2)
                    weights = jnp.exp2((found - new_top) * LOG2)
                    total = state_out[tile, HS : HS + 1, :] * factor + jnp.sum(weights, axis=0, keepdims=True)
                    state_out[tile, HS : HS + 8, :] = jnp.broadcast_to(total, (8, rows))
                    state_out[tile, :HS, :] = state_out[tile, :HS, :] * factor + mixed(value, weights)
                    state_out[tile, HS + 8 :, :] = jnp.broadcast_to(new_top, (8, rows))

                mask_base += keys // sub


def attention(name, query, masks, sub, sources, parts, state=None, small=256):
    tiles, rows, _ = query.shape
    first = state is None
    operands = [query, masks, *sources]
    if not first:
        operands += [state[1], state[0]]
    return pl.pallas_call(
        functools.partial(
            attention_kernel, first=first, count=len(sources), parts=tuple(parts), sub=sub, small=small
        ),
        out_shape=[
            jax.ShapeDtypeStruct((tiles, ROWS, rows), jnp.float32),
            jax.ShapeDtypeStruct((tiles, 8, HS), jnp.float32),
        ],
        input_output_aliases={} if first else {len(operands) - 1: 0},
        cost_estimate=pl.CostEstimate(flops=1024, bytes_accessed=1024, transcendentals=0),
        compiler_params=pltpu.CompilerParams(vmem_limit_bytes=28 * 2**20),
        name=name,
    )(*operands)


def combined(states):
    top = states[0][HS + 8 : HS + 9]
    for state in states[1:]:
        top = jnp.maximum(top, state[HS + 8 : HS + 9])
    total, mixed = 0.0, 0.0
    for state in states:
        factor = jnp.exp2((state[HS + 8 : HS + 9] - top) * LOG2)
        total = total + state[HS : HS + 1] * factor
        mixed = mixed + state[:HS] * factor
    return mixed, total, top


def merge_kernel(*refs):
    *refs, out_ref = refs
    tiles, _, rows = refs[-1].shape
    for tile in range(tiles):
        states = [ref[tile] for ref in refs]
        mixed, total, _ = combined([unspread(a) if a.dtype == jnp.bfloat16 else a for a in states])
        out_ref[tile * rows : (tile + 1) * rows, :] = jnp.transpose(mixed / total).astype(jnp.bfloat16)


def merge(name, *states):
    tiles, _, rows = states[-1].shape
    return pl.pallas_call(
        merge_kernel,
        name=name,
        out_shape=jax.ShapeDtypeStruct((tiles * rows, HS), jnp.bfloat16),
        cost_estimate=pl.CostEstimate(flops=1024, bytes_accessed=1024, transcendentals=0),
        compiler_params=pltpu.CompilerParams(vmem_limit_bytes=32 * 2**20),
    )(*states)


def spread(row):
    parts = []
    for _ in range(3):
        part = row.astype(jnp.bfloat16).astype(jnp.float32)
        parts.append(part)
        row = row - part
    return parts + [jnp.zeros((5, row.shape[1]), jnp.float32)]


def unspread(state):
    state = state.astype(jnp.float32)
    total = state[HS : HS + 1] + state[HS + 1 : HS + 2] + state[HS + 2 : HS + 3]
    top = state[HS + 8 : HS + 9] + state[HS + 9 : HS + 10] + state[HS + 10 : HS + 11]
    return jnp.concatenate([state[:HS], jnp.broadcast_to(total, (8, total.shape[1])), jnp.broadcast_to(top, (8, total.shape[1]))], axis=0)


def fold_kernel(own_ref, other_ref, *out_refs):
    tiles, _, rows = other_ref.shape
    width = out_refs[0].shape[2]
    each = rows // width
    for tile in range(tiles):
        mixed, total, top = combined([own_ref[tile], other_ref[tile]])
        for i in range(each):
            out = out_refs[tile * each + i]
            cut = slice(i * width, (i + 1) * width)
            rows_out = [mixed[:, cut]] + spread(total[:, cut]) + spread(top[:, cut])
            out[0] = jnp.concatenate(rows_out, axis=0).astype(jnp.bfloat16)


def fold(own, other, width):
    tiles, _, rows = other.shape
    return pl.pallas_call(
        fold_kernel,
        name="fold",
        out_shape=[jax.ShapeDtypeStruct((1, ROWS, width), jnp.bfloat16)] * (tiles * rows // width),
        cost_estimate=pl.CostEstimate(flops=1024, bytes_accessed=1024, transcendentals=0),
        compiler_params=pltpu.CompilerParams(vmem_limit_bytes=32 * 2**20),
    )(own, other)


def outgoing_kernel(*refs):
    sources, out_ref = refs[:-1], refs[-1]
    token_rows = sources[0].shape[0]
    piece = token_rows // 4
    at = len(sources) * token_rows
    for z in range(4):
        for yh in range(2):
            for yl in range(2):
                target = (z * 2 + yh) * 2 + yl
                head = 10 * yl + 2 * z + yh
                for i, source in enumerate(sources):
                    out_ref[target, i * token_rows : (i + 1) * token_rows, :] = source[:, head * HS : (head + 1) * HS]
                head = 10 * yl + 8 + yh
                pieces = [
                    source[:, head * HS : (head + 1) * HS].astype(jnp.float32)[z * piece : (z + 1) * piece]
                    for source in sources
                ]
                out_ref[target, at:, :] = jnp.concatenate(pieces, axis=0).astype(jnp.bfloat16)


def outgoing(name, *arrays):
    rows = len(arrays) * arrays[0].shape[0] * 5 // 4
    return pl.pallas_call(
        outgoing_kernel,
        name=name,
        out_shape=jax.ShapeDtypeStruct((16, rows, HS), jnp.bfloat16),
        cost_estimate=pl.CostEstimate(flops=1024, bytes_accessed=1024, transcendentals=0),
        compiler_params=pltpu.CompilerParams(vmem_limit_bytes=16 * 2**20),
    )(*arrays)


def project_kernel(core_ref, att_ref, own_w, side_w, kept_ref, sent_ref):
    core = core_ref[0]
    kept = kept_ref.shape[0]

    def group(number):
        return jnp.concatenate([att_ref[number * 5 + i] for i in range(5)], axis=1)

    total = jnp.dot(group(core), own_w[...], preferred_element_type=jnp.float32)
    total = total + jnp.dot(group(1 - core), side_w[...], preferred_element_type=jnp.float32)
    kept_ref[...] = total[:kept]
    sent_ref[...] = total[kept:].astype(jnp.bfloat16)


def project(core, attended, own_w, side_w, start, columns, width=1280):
    heads, rows, _ = attended.shape
    depth = own_w.shape[0]
    first = start // width
    w_spec = pl.BlockSpec((depth, width), lambda j: (0, j + first))
    out_spec = pl.BlockSpec((rows // 2, width), lambda j: (0, j))
    return pl.pallas_call(
        project_kernel,
        grid=(columns // width,),
        in_specs=[
            pl.BlockSpec(memory_space=pltpu.SMEM),
            pl.BlockSpec((heads, rows, HS), lambda j: (0, 0, 0)),
            w_spec,
            w_spec,
        ],
        out_specs=[out_spec, out_spec],
        out_shape=[
            jax.ShapeDtypeStruct((rows // 2, columns), jnp.float32),
            jax.ShapeDtypeStruct((rows // 2, columns), jnp.bfloat16),
        ],
        cost_estimate=pl.CostEstimate(flops=1024, bytes_accessed=1024, transcendentals=0),
        compiler_params=pltpu.CompilerParams(vmem_limit_bytes=PROJECT_VMEM * 2**20),
        name="project",
    )(core, attended, own_w, side_w)


def finish_kernel(*refs):
    kept, above, below, out_ref = refs[0], refs[1], refs[2], refs[-1]
    half = above.shape[0]
    out_ref[:half, :] = (kept[:half] + above[...].astype(jnp.float32)).astype(jnp.bfloat16)
    out_ref[half:, :] = (kept[half:] + below[...].astype(jnp.float32)).astype(jnp.bfloat16)


def finish(index, parts, whole=None):
    rows, columns = parts[0].shape
    half = rows // 2
    specs = [pl.BlockSpec((rows, columns), lambda i: (0, 0))] + [pl.BlockSpec((half, columns), lambda i: (0, 0))] * 2
    operands = list(parts)
    if whole is not None:
        specs.append(pl.BlockSpec(memory_space=pl.ANY))
        operands.append(whole)
    return pl.pallas_call(
        finish_kernel,
        name="finish",
        grid=(1,),
        in_specs=specs,
        out_specs=pl.BlockSpec((rows, columns), lambda i: (0, index)),
        out_shape=jax.ShapeDtypeStruct((rows, columns * CHUNKS), jnp.bfloat16),
        input_output_aliases={} if whole is None else {3: 0},
        compiler_params=pltpu.CompilerParams(vmem_limit_bytes=16 * 2**20),
    )(*operands)


def ring(array, axes, size, shift, name="ring"):
    with jax.named_scope(name):
        return lax.ppermute(array, axes, [(i, (i + shift) % size) for i in range(size)])


def cross(array, axis, bit, name):
    with jax.named_scope(name):
        return lax.ppermute(array, axis, [(i, i ^ bit) for i in range(4)])


def swap(array, name="swap"):
    with jax.named_scope(name):
        return lax.ppermute(array, "c", [(0, 1), (1, 0)])


def mask_tables(block_mask, frame_map):
    x, z, core = lax.axis_index("x"), lax.axis_index("z"), lax.axis_index("c")
    low, group = np.arange(2)[None, :, None], np.arange(3)
    at_core = np.arange(2)[:, None, None]
    ring_within = ((low * 2 + at_core) * 96 + group * 32) // BLOCK
    at_z = np.arange(4)[:, None, None, None]
    plane_within = ((low * 2 + at_core) * 96 + at_z * 24 + group * 8) // BLOCK

    def frames(at_x):
        return lax.dynamic_slice_in_dim(frame_map, at_x * 8, 8)[:, None, None] * FB

    def ring_blocks(at_x, at_core):
        within = jnp.asarray(ring_within.astype(np.int32))[at_core]
        return (frames(at_x) + within[None]).reshape(-1)

    def plane_blocks(at_x, at_core, at_z):
        within = jnp.asarray(plane_within.astype(np.int32))[at_z, at_core]
        return (frames(at_x) + within[None]).reshape(-1)

    ring_keys = jnp.concatenate([ring_blocks((x + i) % 4, core) for i in NEAR])
    plane_keys = jnp.concatenate([plane_blocks(x, core, z ^ i) for i in range(4)])
    blocks = jnp.arange(block_mask.shape[0], dtype=jnp.int32)
    pad = jnp.zeros((32,), jnp.int32)
    ring_queries, plane_queries = [], []
    for side in (0, 1):
        ring_queries += [ring_blocks(x, core ^ side), pad, pad, pad[:16]]
        for pair in (0, 2):
            plane_queries += [plane_blocks(x ^ (pair + i), core ^ side, z) for i in (0, 1)] + [pad]
    blocked = (block_mask <= 0).astype(jnp.bfloat16)

    def pick(index):
        return (index[:, None] == blocks[None, :]).astype(jnp.bfloat16)

    queries = pick(jnp.concatenate(ring_queries + plane_queries))
    by_query = jnp.dot(queries, blocked, preferred_element_type=jnp.float32).astype(jnp.bfloat16).reshape(6, HS, -1)

    def table(index, part):
        found = jnp.einsum("kb,tcb->tkc", pick(index), part, preferred_element_type=jnp.float32)
        return found * NEG

    return table(ring_keys, by_query[:2]), table(plane_keys, by_query[2:])


def local(queries, keys, values, w_out, block_mask, frame_map):
    core = lax.axis_index("c").astype(jnp.int32)
    z, low = lax.axis_index("z"), lax.axis_index("yl")
    token_rows = queries.shape[0]
    piece = token_rows // 4

    side_w = swap(w_out, "side_w")
    with jax.named_scope("spread"):
        sent = lax.all_to_all(outgoing("outgoing", keys, values, queries), RING, 0, 0)
    one, two, three = token_rows, 2 * token_rows, 3 * token_rows
    ring_kv = jnp.concatenate([sent[:, :one], sent[:, one:two]], axis=0).reshape(-1, HS)
    ring_q = sent[:, two:three].reshape(-1, HS)
    plane_kv = jnp.concatenate([sent[:, three : three + piece], sent[:, three + piece : three + 2 * piece]], axis=0)
    plane_kv = plane_kv.reshape(-1, HS)
    plane_q = sent[:, three + 2 * piece :].reshape(-1, HS)
    ring_rows = 16 * token_rows
    plane_rows = 16 * piece

    ring_masks, plane_masks = mask_tables(block_mask, frame_map)

    side_w, ring_kv, ring_q, plane_kv, plane_q = lax.optimization_barrier((side_w, ring_kv, ring_q, plane_kv, plane_q))
    ring_left, ring_right = ring(ring_kv, "x", 4, 1, "ring_x"), ring(ring_kv, "x", 4, -1, "ring_x")
    query_a = jnp.stack([ring_q, swap(ring_q, "swap_q")])

    plane_kv = [plane_kv] + [cross(plane_kv, "z", i, "plane_z") for i in (1, 2, 3)]
    plane_q = jnp.concatenate([plane_q] + [cross(plane_q, "x", i, "plane_q") for i in (1, 2, 3)], axis=0)
    query_b = jnp.concatenate([plane_q, swap(plane_q, "swap_plane_q")], axis=0).reshape(4, 2 * plane_rows, HS)
    query_a, query_b = lax.optimization_barrier((query_a, query_b))
    whole = [(0, 0, 0, ring_rows, ring_rows)]
    state = attention("own", query_a, ring_masks[:, :48], 32, [ring_kv], whole)
    plane_parts = [(i, 0, i, plane_rows, plane_rows) for i in range(4)]
    query_b, state = lax.optimization_barrier((query_b, state))
    plane_state = attention("plane", query_b, plane_masks, 8, plane_kv, plane_parts, small=128)

    plane_state, ring_left, ring_right = lax.optimization_barrier((plane_state, ring_left, ring_right))
    other_b = swap(plane_state[0][2:], "swap_b")
    plane_part = fold(plane_state[0], other_b, plane_rows)
    plane_part, state, ring_left, ring_right = lax.optimization_barrier((plane_part, state, ring_left, ring_right))
    middle = ring_kv.shape[0] // 2
    ring_far = [
        ring(ring_left[:middle], "x", 4, 1, "ring_x_far"),
        ring(ring_right[middle:], "x", 4, -1, "ring_x_far"),
    ]
    plane_part = [plane_part[0]] + [cross(plane_part[i], "x", i, "plane_sum") for i in (1, 2, 3)]
    state = attention("left", query_a, ring_masks[:, 48:96], 32, [ring_left], whole, state)
    state = attention("right", query_a, ring_masks[:, 96:144], 32, [ring_right], whole, state)
    out_b = merge("merge_plane", *plane_part).reshape(4, 2, 2, piece, HS)
    out_b, state = lax.optimization_barrier((out_b, state))
    far = [(0, 0, 1, 0, ring_rows)]
    side = attention(
        "far_side", query_a[1:], ring_masks[1:, 144:], 32, ring_far, far, (state[0][1:], state[1][1:])
    )
    other_a = swap(side[0], "swap_a")
    state, side = lax.optimization_barrier((state, side))
    state = attention("far_own", query_a[:1], ring_masks[:1, 144:], 32, ring_far, far, (state[0][:1], state[1][:1]))
    out_a = merge("merge_ring", state[0], other_a).reshape(4, 2, 2, token_rows, HS)

    def split(array):
        first, second = array[:, :, 0], array[:, :, 1]
        same = jnp.where(low == 0, first, second)
        other = jnp.where(low == 0, second, first)
        flipped = jnp.stack([other[:, 1], other[:, 0]], axis=1)
        below = jnp.where(low == 0, flipped, other)
        above = jnp.where(low == 0, other, flipped)
        return same, below, above

    half = token_rows // 2
    same, below, above = split(out_a)
    piece_same, piece_below, piece_above = split(out_b)
    back = jnp.concatenate(
        [same, below[:, :, :half], above[:, :, half:], piece_same, jnp.where(z < 2, piece_below, piece_above)], axis=2
    ).reshape(8, -1, HS)
    with jax.named_scope("return"):
        back = lax.all_to_all(back, ("z", "yh"), 0, 0)
    rows = 2 * token_rows
    plane_back = back[:, rows:].reshape(4, 2, 2, piece, HS).transpose(1, 2, 0, 3, 4).reshape(2, rows, HS)
    attended = jnp.concatenate([back[:, :rows], plane_back], axis=0)

    out = None
    columns = w_out.shape[1] // CHUNKS
    for i in range(CHUNKS):
        kept, sent = project(core[None], attended, w_out, side_w, i * columns, columns)
        from_above = ring(sent[:half], Y, 4, -1, "sum_y")
        from_below = ring(sent[half:], Y, 4, 1, "sum_y")
        out = finish(i, (kept, from_above, from_below), out)
    return out


def solution(mesh):
    fine = jax.sharding.Mesh(mesh.devices.reshape(4, 4, 2, 2, 2), ALL)
    rows = P(ALL, None)
    placed = (rows, rows, rows, P(("yl", "c"), None), P(), P())
    return jax.shard_map(local, mesh=fine, in_specs=placed, out_specs=rows, check_vma=False)
```

```python
import functools

import jax
import jax.numpy as jnp
import numpy as np
from jax import lax
from jax.experimental import pallas as pl
from jax.experimental.pallas import tpu as pltpu
from jax.sharding import PartitionSpec as P

HS = 128
BLOCK = 64
FRAME = 384
FB = FRAME // BLOCK
NEG = -1e30
SCALE = HS ** -0.5
LOG2 = float(SCALE * np.log2(np.e))
BOUND = 60.0

RING = ("z", "yh", "yl")
Y = ("yh", "yl")
ALL = ("x", "z", "yh", "yl", "c")
WIDTH = 1280
CHUNKS = 2
NEAR = (0, 3, 1, 2)
ROWS = 144


def square_norm_max(rows):
    wide = rows.astype(jnp.float32)
    return jnp.max(jnp.sum(wide * wide, axis=1, keepdims=True))


def attention_kernel(*refs, first, count, parts, sub, small, skip):
    q_ref, mt_ref = refs[0], refs[1]
    sources = refs[2 : 2 + count]
    if first:
        state_in = norm_in = None
        state_out, norm_out = refs[2 + count :]
    else:
        norm_in, state_in, state_out, norm_out = refs[2 + count :]
    _, rows, _ = q_ref.shape

    def joined(slices):
        return slices[0] if len(slices) == 1 else jnp.concatenate(slices, axis=0)

    def with_masks(key, tile, mask_at, size):
        masks = mt_ref[tile, pl.ds(mask_at, size // sub), :]
        masks = jnp.broadcast_to(masks[:, None, :], (size // sub, sub, HS)).reshape(size, HS)
        return jnp.concatenate([key, masks.astype(jnp.bfloat16)], axis=1)

    def scores(key, query):
        return lax.dot_general(key, query, (((1,), (1,)), ((), ())), preferred_element_type=jnp.float32)

    def mixed(value, weights):
        return lax.dot_general(
            value, weights.astype(jnp.bfloat16), (((0,), (0,)), ((), ())), preferred_element_type=jnp.float32
        )

    key_norm = jnp.float32(0.0)
    for k_source, k_at, _, _, keys in parts:
        key_norm = jnp.maximum(key_norm, square_norm_max(sources[k_source][k_at : k_at + keys, :]))
    all_keys = sum(part[4] for part in parts)

    @pl.loop(0, state_out.shape[0])
    def _(at_tile):
        tile = at_tile + skip
        query_norm = square_norm_max(q_ref[tile]) if first else jnp.max(norm_in[tile])
        bounded = jnp.logical_and(query_norm >= 0.0, query_norm * key_norm <= (BOUND / SCALE) ** 2)
        place = lax.broadcasted_iota(jnp.int32, (rows, HS), 0) // sub
        one_hot = jnp.where(place == lax.broadcasted_iota(jnp.int32, (rows, HS), 1), 1.0, 0.0).astype(jnp.bfloat16)
        query = jnp.concatenate([q_ref[tile], one_hot], axis=1)
        norm_out[at_tile] = jnp.full((8, HS), jnp.where(bounded, query_norm, -1.0), jnp.float32)

        @pl.when(bounded)
        def _():
            key = joined([sources[k][at : at + keys, :] for k, at, _, _, keys in parts])
            value = joined([sources[v][at : at + keys, :] for _, _, v, at, keys in parts])
            weights = jnp.exp2(scores(with_masks(key, tile, 0, all_keys), query) * LOG2)
            total = jnp.sum(weights, axis=0, keepdims=True)
            weighted = mixed(value, weights)
            if not first:
                total = state_in[tile, HS : HS + 1, :] + total
                weighted = state_in[tile, :HS, :] + weighted
            state_out[at_tile, :HS, :] = weighted
            state_out[at_tile, HS : HS + 8, :] = jnp.broadcast_to(total, (8, rows))
            state_out[at_tile, HS + 8 :, :] = jnp.zeros((8, rows), jnp.float32)

        @pl.when(jnp.logical_not(bounded))
        def _():
            if first:
                state_out[at_tile, : HS + 8, :] = jnp.zeros((HS + 8, rows), jnp.float32)
                state_out[at_tile, HS + 8 :, :] = jnp.full((8, rows), NEG, jnp.float32)
            else:
                state_out[at_tile] = state_in[tile]
            mask_base = 0
            for k_source, k_at, v_source, v_at, keys in parts:

                @pl.loop(0, keys // small)
                def _(j):
                    key = sources[k_source][pl.ds(pl.multiple_of(k_at + j * small, small), small), :]
                    value = sources[v_source][pl.ds(pl.multiple_of(v_at + j * small, small), small), :]
                    mask_at = pl.multiple_of(mask_base + j * (small // sub), 8)
                    found = scores(with_masks(key, tile, mask_at, small), query)
                    top = state_out[at_tile, HS + 8 : HS + 9, :]
                    new_top = jnp.maximum(top, jnp.max(found, axis=0, keepdims=True))
                    factor = jnp.exp2((top - new_top) * LOG2)
                    weights = jnp.exp2((found - new_top) * LOG2)
                    total = state_out[at_tile, HS : HS + 1, :] * factor + jnp.sum(weights, axis=0, keepdims=True)
                    state_out[at_tile, HS : HS + 8, :] = jnp.broadcast_to(total, (8, rows))
                    state_out[at_tile, :HS, :] = state_out[at_tile, :HS, :] * factor + mixed(value, weights)
                    state_out[at_tile, HS + 8 :, :] = jnp.broadcast_to(new_top, (8, rows))

                mask_base += keys // sub


def attention(name, query, masks, sub, sources, parts, state=None, small=256, skip=0, tiles=None, cost=1024):
    rows = query.shape[1]
    first, whole = state is None, tiles is None
    tiles = query.shape[0] if whole else tiles
    operands = [query, masks, *sources]
    if not first:
        operands += [state[1], state[0]]
    return pl.pallas_call(
        functools.partial(
            attention_kernel, first=first, count=len(sources), parts=tuple(parts), sub=sub, small=small, skip=skip
        ),
        out_shape=[
            jax.ShapeDtypeStruct((tiles, ROWS, rows), jnp.float32),
            jax.ShapeDtypeStruct((tiles, 8, HS), jnp.float32),
        ],
        input_output_aliases={} if first or not whole else {len(operands) - 1: 0},
        cost_estimate=pl.CostEstimate(flops=cost, bytes_accessed=1024, transcendentals=0),
        compiler_params=pltpu.CompilerParams(vmem_limit_bytes=20 * 2**20),
        name=name,
    )(*operands)


def combined(states):
    top = states[0][HS + 8 : HS + 9]
    for state in states[1:]:
        top = jnp.maximum(top, state[HS + 8 : HS + 9])
    total, mixed = 0.0, 0.0
    for state in states:
        factor = jnp.exp2((state[HS + 8 : HS + 9] - top) * LOG2)
        total = total + state[HS : HS + 1] * factor
        mixed = mixed + state[:HS] * factor
    return mixed, total, top


def merge_kernel(*refs):
    *refs, out_ref = refs
    tiles, _, rows = refs[-1].shape
    for tile in range(tiles):
        states = [ref[tile] for ref in refs]
        mixed, total, _ = combined([unspread(a) if a.dtype == jnp.bfloat16 else a for a in states])
        out_ref[tile * rows : (tile + 1) * rows, :] = jnp.transpose(mixed / total).astype(jnp.bfloat16)


def merge(name, *states, cost=1024):
    tiles, _, rows = states[-1].shape
    return pl.pallas_call(
        merge_kernel,
        name=name,
        out_shape=jax.ShapeDtypeStruct((tiles * rows, HS), jnp.bfloat16),
        cost_estimate=pl.CostEstimate(flops=cost, bytes_accessed=1024, transcendentals=0),
        compiler_params=pltpu.CompilerParams(vmem_limit_bytes=32 * 2**20),
    )(*states)


def spread(row):
    parts = []
    for _ in range(3):
        part = row.astype(jnp.bfloat16).astype(jnp.float32)
        parts.append(part)
        row = row - part
    return parts + [jnp.zeros((5, row.shape[1]), jnp.float32)]


def unspread(state):
    state = state.astype(jnp.float32)
    total = state[HS : HS + 1] + state[HS + 1 : HS + 2] + state[HS + 2 : HS + 3]
    top = state[HS + 8 : HS + 9] + state[HS + 9 : HS + 10] + state[HS + 10 : HS + 11]
    return jnp.concatenate([state[:HS], jnp.broadcast_to(total, (8, total.shape[1])), jnp.broadcast_to(top, (8, total.shape[1]))], axis=0)


def fold_kernel(own_ref, other_ref, *out_refs):
    tiles, _, rows = other_ref.shape
    width = out_refs[0].shape[2]
    each = rows // width
    for tile in range(tiles):
        mixed, total, top = combined([own_ref[tile], other_ref[tile]])
        for i in range(each):
            out = out_refs[tile * each + i]
            cut = slice(i * width, (i + 1) * width)
            rows_out = [mixed[:, cut]] + spread(total[:, cut]) + spread(top[:, cut])
            out[0] = jnp.concatenate(rows_out, axis=0).astype(jnp.bfloat16)


def fold(own, other, width):
    tiles, _, rows = other.shape
    return pl.pallas_call(
        fold_kernel,
        name="fold",
        out_shape=[jax.ShapeDtypeStruct((1, ROWS, width), jnp.bfloat16)] * (tiles * rows // width),
        cost_estimate=pl.CostEstimate(flops=1024, bytes_accessed=1024, transcendentals=0),
        compiler_params=pltpu.CompilerParams(vmem_limit_bytes=32 * 2**20),
    )(own, other)


def outgoing_kernel(*refs):
    *sources, out_ref, held, semaphores = refs
    count = len(sources)
    token_rows = sources[0].shape[0]
    piece = token_rows // 4
    at = count * token_rows
    copies = [pltpu.make_async_copy(source, held.at[i], semaphores.at[i]) for i, source in enumerate(sources)]
    for copy in copies:
        copy.start()
    chips = [(z, yh, yl) for z in range(4) for yh in range(2) for yl in range(2)]
    for i, copy in enumerate(copies):
        copy.wait()
        for z, yh, yl in chips:
            head = 10 * yl + 2 * z + yh
            target = (z * 2 + yh) * 2 + yl
            out_ref[target, i * token_rows : (i + 1) * token_rows, :] = held[i, :, head * HS : (head + 1) * HS]
    for z, yh, yl in chips:
        head = 10 * yl + 8 + yh
        pieces = [
            held[i, :, head * HS : (head + 1) * HS].astype(jnp.float32)[z * piece : (z + 1) * piece] for i in range(count)
        ]
        out_ref[(z * 2 + yh) * 2 + yl, at:, :] = jnp.concatenate(pieces, axis=0).astype(jnp.bfloat16)


def outgoing(name, *arrays):
    rows = len(arrays) * arrays[0].shape[0] * 5 // 4
    return pl.pallas_call(
        outgoing_kernel,
        name=name,
        in_specs=[pl.BlockSpec(memory_space=pl.ANY)] * len(arrays),
        out_shape=jax.ShapeDtypeStruct((16, rows, HS), jnp.bfloat16),
        scratch_shapes=[
            pltpu.VMEM((len(arrays), *arrays[0].shape), jnp.bfloat16),
            pltpu.SemaphoreType.DMA((len(arrays),)),
        ],
        cost_estimate=pl.CostEstimate(flops=1024, bytes_accessed=1024, transcendentals=0),
        compiler_params=pltpu.CompilerParams(vmem_limit_bytes=60 * 2**20),
    )(*arrays)


def project_kernel(core_ref, att_ref, own_w, side_w, kept_ref, above_ref, below_ref, held, semaphores, *, start):
    core = core_ref[0]
    kept, half = kept_ref.shape[0], above_ref.shape[0]
    steps = kept_ref.shape[1] // WIDTH

    def columns(j, base=0):
        return pl.ds(pl.multiple_of(base + j * WIDTH, HS), WIDTH)

    def arriving(j):
        return pltpu.make_async_copy(side_w.at[:, columns(j, start)], held.at[j], semaphores.at[j])

    for j in range(steps):
        arriving(j).start()

    def group(number):
        return jnp.concatenate([att_ref[number * 5 + i] for i in range(5)], axis=1)

    own, side = group(core), group(1 - core)

    @pl.loop(0, steps)
    def _(j):
        total = jnp.dot(own, own_w[:, columns(j, start)], preferred_element_type=jnp.float32)
        arriving(j).wait()
        total = total + jnp.dot(side, held[j], preferred_element_type=jnp.float32)
        kept_ref[:, columns(j)] = total[:kept].astype(jnp.bfloat16)
        above_ref[:, columns(j)] = total[kept : kept + half].astype(jnp.bfloat16)
        below_ref[:, columns(j)] = total[kept + half :].astype(jnp.bfloat16)


def project(core, attended, own_w, side_w, start, columns):
    rows, steps = attended.shape[1], columns // WIDTH
    return pl.pallas_call(
        functools.partial(project_kernel, start=start),
        name="project",
        in_specs=[
            pl.BlockSpec(memory_space=pltpu.SMEM),
            pl.BlockSpec(memory_space=pltpu.VMEM),
            pl.BlockSpec(memory_space=pltpu.VMEM),
            pl.BlockSpec(memory_space=pl.ANY),
        ],
        out_shape=[
            jax.ShapeDtypeStruct((rows // 2, columns), jnp.bfloat16),
            jax.ShapeDtypeStruct((rows // 4, columns), jnp.bfloat16),
            jax.ShapeDtypeStruct((rows // 4, columns), jnp.bfloat16),
        ],
        scratch_shapes=[
            pltpu.VMEM((steps, side_w.shape[0], WIDTH), jnp.bfloat16),
            pltpu.SemaphoreType.DMA((steps,)),
        ],
        cost_estimate=pl.CostEstimate(flops=1024, bytes_accessed=1024, transcendentals=0),
        compiler_params=pltpu.CompilerParams(vmem_limit_bytes=24 * 2**20),
    )(core, attended, own_w, side_w)


def ring(array, axes, size, shift, name="ring"):
    with jax.named_scope(name):
        return lax.ppermute(array, axes, [(i, (i + shift) % size) for i in range(size)])


def cross(array, axis, bit, name):
    with jax.named_scope(name):
        return lax.ppermute(array, axis, [(i, i ^ bit) for i in range(4)])


def swap(array, name="swap"):
    with jax.named_scope(name):
        return lax.ppermute(array, "c", [(0, 1), (1, 0)])


def mask_tables(block_mask, frame_map):
    x, z, core = lax.axis_index("x"), lax.axis_index("z"), lax.axis_index("c")
    low, group = np.arange(2)[None, :, None], np.arange(3)
    at_core = np.arange(2)[:, None, None]
    ring_within = ((low * 2 + at_core) * 96 + group * 32) // BLOCK
    at_z = np.arange(4)[:, None, None, None]
    plane_within = ((low * 2 + at_core) * 96 + at_z * 24 + group * 8) // BLOCK

    def frames(at_x):
        return lax.dynamic_slice_in_dim(frame_map, at_x * 8, 8)[:, None, None] * FB

    def ring_blocks(at_x, at_core):
        within = jnp.asarray(ring_within.astype(np.int32))[at_core]
        return (frames(at_x) + within[None]).reshape(-1)

    def plane_blocks(at_x, at_core, at_z):
        within = jnp.asarray(plane_within.astype(np.int32))[at_z, at_core]
        return (frames(at_x) + within[None]).reshape(-1)

    ring_keys = jnp.concatenate([ring_blocks((x + i) % 4, core) for i in NEAR])
    plane_keys = jnp.concatenate([plane_blocks(x, core, z ^ i) for i in (0, 2, 1, 3)])
    blocks = jnp.arange(block_mask.shape[0], dtype=jnp.int32)
    pad = jnp.zeros((32,), jnp.int32)
    ring_queries, plane_queries = [], []
    for side in (0, 1):
        ring_queries += [ring_blocks(x, core ^ side), pad, pad, pad[:16]]
        for pair in (0, 2):
            plane_queries += [plane_blocks(x ^ (pair + i), core ^ side, z) for i in (0, 1)] + [pad]
    blocked = (block_mask <= 0).astype(jnp.bfloat16)

    def pick(index):
        return (index[:, None] == blocks[None, :]).astype(jnp.bfloat16)

    queries = pick(jnp.concatenate(ring_queries + plane_queries))
    by_query = jnp.dot(queries, blocked, preferred_element_type=jnp.float32).astype(jnp.bfloat16).reshape(6, HS, -1)

    def table(index, part):
        found = jnp.einsum("kb,tcb->tkc", pick(index), part, preferred_element_type=jnp.float32)
        return found * NEG

    return table(ring_keys, by_query[:2]), table(plane_keys, by_query[2:])


def local(queries, keys, values, w_out, block_mask, frame_map):
    core = lax.axis_index("c").astype(jnp.int32)
    z, low = lax.axis_index("z"), lax.axis_index("yl")
    token_rows = queries.shape[0]
    piece = token_rows // 4

    side_w = swap(w_out, "side_w")
    with jax.named_scope("spread"):
        sent = lax.all_to_all(outgoing("outgoing", keys, values, queries), RING, 0, 0)
    one, two, three = token_rows, 2 * token_rows, 3 * token_rows
    ring_kv = jnp.concatenate([sent[:, :one], sent[:, one:two]], axis=0).reshape(-1, HS)
    ring_q = sent[:, two:three].reshape(-1, HS)
    plane_kv = jnp.concatenate([sent[:, three : three + piece], sent[:, three + piece : three + 2 * piece]], axis=0)
    plane_kv = plane_kv.reshape(-1, HS)
    plane_q = sent[:, three + 2 * piece :].reshape(-1, HS)
    ring_rows = 16 * token_rows
    plane_rows = 16 * piece

    ring_masks, plane_masks = mask_tables(block_mask, frame_map)

    side_w, ring_kv, ring_q, plane_kv, plane_q = lax.optimization_barrier((side_w, ring_kv, ring_q, plane_kv, plane_q))
    ring_left, ring_right = ring(ring_kv, "x", 4, 1, "ring_x"), ring(ring_kv, "x", 4, -1, "ring_x")
    query_a = jnp.stack([ring_q, swap(ring_q, "swap_q")])

    plane_kv = [plane_kv] + [cross(plane_kv, "z", i, "plane_z") for i in (2, 1, 3)]
    plane_q = jnp.concatenate([plane_q] + [cross(plane_q, "x", i, "plane_q") for i in (1, 2, 3)], axis=0)
    query_b = jnp.concatenate([plane_q, swap(plane_q, "swap_plane_q")], axis=0).reshape(4, 2 * plane_rows, HS)
    query_a, query_b = lax.optimization_barrier((query_a, query_b))
    whole = [(0, 0, 0, ring_rows, ring_rows)]
    state = attention("own", query_a, ring_masks[:, :48], 32, [ring_kv], whole)
    plane_parts = [(i, 0, i, plane_rows, plane_rows) for i in range(4)]
    query_b, state = lax.optimization_barrier((query_b, state))
    plane_state = attention("plane", query_b, plane_masks, 8, plane_kv, plane_parts, small=128)

    plane_state, state, ring_left, ring_right = lax.optimization_barrier((plane_state, state, ring_left, ring_right))
    other_b = swap(plane_state[0][2:], "swap_b")
    middle = ring_kv.shape[0] // 2
    ring_far = [
        ring(ring_left[:middle], "x", 4, 1, "ring_x_far"),
        ring(ring_right[middle:], "x", 4, -1, "ring_x_far"),
    ]
    state = attention("left", query_a, ring_masks[:, 48:96], 32, [ring_left], whole, state)
    own_part, other_b, state = lax.optimization_barrier((plane_state[0], other_b, state))
    plane_part = fold(own_part, other_b, plane_rows)
    plane_part, state = lax.optimization_barrier((plane_part, state))
    plane_part = [plane_part[0]] + [cross(plane_part[i], "x", i, "plane_sum") for i in (1, 2, 3)]
    state = attention("right", query_a, ring_masks[:, 96:144], 32, [ring_right], whole, state)
    out_b = merge("merge_plane", *plane_part).reshape(4, 2, 2, piece, HS)
    out_b, state = lax.optimization_barrier((out_b, state))
    far = [(0, 0, 1, 0, ring_rows)]
    far_masks = ring_masks[:, 144:]
    side = attention("far_side", query_a, far_masks, 32, ring_far, far, state, skip=1, tiles=1)
    other_a = swap(side[0], "swap_a")
    state, side = lax.optimization_barrier((state, side))
    own = attention("far_own", query_a, far_masks, 32, ring_far, far, state, skip=0, tiles=1)
    out_a = merge("merge_ring", own[0], other_a, cost=1 << 32).reshape(4, 2, 2, token_rows, HS)

    def split(array):
        first, second = array[:, :, 0], array[:, :, 1]
        same = jnp.where(low == 0, first, second)
        other = jnp.where(low == 0, second, first)
        flipped = jnp.stack([other[:, 1], other[:, 0]], axis=1)
        below = jnp.where(low == 0, flipped, other)
        above = jnp.where(low == 0, other, flipped)
        return same, below, above

    half = token_rows // 2
    same, below, above = split(out_a)
    piece_same, piece_below, piece_above = split(out_b)
    back = jnp.concatenate(
        [same, below[:, :, :half], above[:, :, half:], piece_same, jnp.where(z < 2, piece_below, piece_above)], axis=2
    ).reshape(8, -1, HS)
    with jax.named_scope("return"):
        back = lax.all_to_all(back, ("z", "yh"), 0, 0)
    rows = 2 * token_rows
    plane_back = back[:, rows:].reshape(4, 2, 2, piece, HS).transpose(1, 2, 0, 3, 4).reshape(2, rows, HS)
    attended = jnp.concatenate([back[:, :rows], plane_back], axis=0)

    outs = []
    columns = w_out.shape[1] // CHUNKS
    for i in range(CHUNKS):
        kept, to_below, to_above = project(core[None], attended, w_out, side_w, i * columns, columns)
        from_above, from_below = ring(to_below, Y, 4, -1, "sum_y"), ring(to_above, Y, 4, 1, "sum_y")
        other = jnp.concatenate([from_above, from_below], axis=0)
        out = (kept.astype(jnp.float32) + other.astype(jnp.float32)).astype(jnp.bfloat16)
        outs.append(out if i == CHUNKS - 1 else lax.optimization_barrier(out))
    return outs[0] if CHUNKS == 1 else jnp.concatenate(outs, axis=1)


def solution(mesh):
    fine = jax.sharding.Mesh(mesh.devices.reshape(4, 4, 2, 2, 2), ALL)
    rows = P(ALL, None)
    placed = (rows, rows, rows, P(("yl", "c"), None), P(), P())
    return jax.shard_map(local, mesh=fine, in_specs=placed, out_specs=rows, check_vma=False)
```

```python
import functools

import jax
import jax.numpy as jnp
import numpy as np
from jax import lax
from jax.experimental import pallas as pl
from jax.experimental.pallas import tpu as pltpu
from jax.sharding import PartitionSpec as P

HS = 128
BLOCK = 64
FRAME = 384
FB = FRAME // BLOCK
NEG = -1e30
SCALE = HS ** -0.5
LOG2 = float(SCALE * np.log2(np.e))
BOUND = 60.0

RING = ("z", "yh", "yl")
Y = ("yh", "yl")
ALL = ("x", "z", "yh", "yl", "c")
WIDTH = 1280
CHUNKS = 2
NEAR = (0, 3, 1, 2)
ROWS = 144


def square_norm_max(rows):
    wide = rows.astype(jnp.float32)
    return jnp.max(jnp.sum(wide * wide, axis=1, keepdims=True))


def attention_kernel(*refs, first, count, parts, sub, small, skip):
    q_ref, mt_ref = refs[0], refs[1]
    sources = refs[2 : 2 + count]
    if first:
        state_in = norm_in = None
        state_out, norm_out = refs[2 + count :]
    else:
        norm_in, state_in, state_out, norm_out = refs[2 + count :]
    _, rows, _ = q_ref.shape

    def joined(slices):
        return slices[0] if len(slices) == 1 else jnp.concatenate(slices, axis=0)

    def with_masks(key, tile, mask_at, size):
        masks = mt_ref[tile, pl.ds(mask_at, size // sub), :]
        masks = jnp.broadcast_to(masks[:, None, :], (size // sub, sub, HS)).reshape(size, HS)
        return jnp.concatenate([key, masks.astype(jnp.bfloat16)], axis=1)

    def scores(key, query):
        return lax.dot_general(key, query, (((1,), (1,)), ((), ())), preferred_element_type=jnp.float32)

    def mixed(value, weights):
        return lax.dot_general(
            value, weights.astype(jnp.bfloat16), (((0,), (0,)), ((), ())), preferred_element_type=jnp.float32
        )

    all_keys = sum(part[4] for part in parts)

    @pl.loop(0, state_out.shape[0])
    def _(at_tile):
        tile = at_tile + skip
        place = lax.broadcasted_iota(jnp.int32, (rows, HS), 0) // sub
        one_hot = jnp.where(place == lax.broadcasted_iota(jnp.int32, (rows, HS), 1), 1.0, 0.0).astype(jnp.bfloat16)
        query = jnp.concatenate([q_ref[tile], one_hot], axis=1)
        key = joined([sources[k][at : at + keys, :] for k, at, _, _, keys in parts])
        value = joined([sources[v][at : at + keys, :] for _, _, v, at, keys in parts])
        weights = jnp.exp2(scores(with_masks(key, tile, 0, all_keys), query) * LOG2)
        total = jnp.sum(weights, axis=0, keepdims=True)
        weighted = mixed(value, weights)
        if not first:
            total = state_in[tile, HS : HS + 1, :] + total
            weighted = state_in[tile, :HS, :] + weighted
        state_out[at_tile, :HS, :] = weighted
        state_out[at_tile, HS : HS + 8, :] = jnp.broadcast_to(total, (8, rows))
        state_out[at_tile, HS + 8 :, :] = jnp.broadcast_to(jnp.where(total > 0.0, 0.0, NEG), (8, rows))

        query_norm = square_norm_max(q_ref[tile]) if first else jnp.max(norm_in[tile])
        bounded = jnp.logical_and(query_norm >= 0.0, query_norm * square_norm_max(key) <= (BOUND / SCALE) ** 2)
        norm_out[at_tile] = jnp.full((8, HS), jnp.where(bounded, query_norm, -1.0), jnp.float32)

        @pl.when(jnp.logical_not(bounded))
        def _():
            if first:
                state_out[at_tile, : HS + 8, :] = jnp.zeros((HS + 8, rows), jnp.float32)
                state_out[at_tile, HS + 8 :, :] = jnp.full((8, rows), NEG, jnp.float32)
            else:
                state_out[at_tile] = state_in[tile]
            mask_base = 0
            for k_source, k_at, v_source, v_at, keys in parts:

                @pl.loop(0, keys // small)
                def _(j):
                    key = sources[k_source][pl.ds(pl.multiple_of(k_at + j * small, small), small), :]
                    value = sources[v_source][pl.ds(pl.multiple_of(v_at + j * small, small), small), :]
                    mask_at = pl.multiple_of(mask_base + j * (small // sub), 8)
                    found = scores(with_masks(key, tile, mask_at, small), query)
                    top = state_out[at_tile, HS + 8 : HS + 9, :]
                    new_top = jnp.maximum(top, jnp.max(found, axis=0, keepdims=True))
                    factor = jnp.exp2((top - new_top) * LOG2)
                    weights = jnp.exp2((found - new_top) * LOG2)
                    total = state_out[at_tile, HS : HS + 1, :] * factor + jnp.sum(weights, axis=0, keepdims=True)
                    state_out[at_tile, HS : HS + 8, :] = jnp.broadcast_to(total, (8, rows))
                    state_out[at_tile, :HS, :] = state_out[at_tile, :HS, :] * factor + mixed(value, weights)
                    state_out[at_tile, HS + 8 :, :] = jnp.broadcast_to(new_top, (8, rows))

                mask_base += keys // sub


def attention(name, query, masks, sub, sources, parts, state=None, small=256, skip=0, tiles=None, cost=1024):
    rows = query.shape[1]
    first = state is None
    tiles = query.shape[0] if tiles is None else tiles
    operands = [query, masks, *sources]
    if not first:
        operands += [state[1], state[0]]
    return pl.pallas_call(
        functools.partial(
            attention_kernel, first=first, count=len(sources), parts=tuple(parts), sub=sub, small=small, skip=skip
        ),
        out_shape=[
            jax.ShapeDtypeStruct((tiles, ROWS, rows), jnp.float32),
            jax.ShapeDtypeStruct((tiles, 8, HS), jnp.float32),
        ],
        cost_estimate=pl.CostEstimate(flops=cost, bytes_accessed=1024, transcendentals=0),
        compiler_params=pltpu.CompilerParams(vmem_limit_bytes=20 * 2**20),
        name=name,
    )(*operands)


def combined(states):
    top = states[0][HS + 8 : HS + 9]
    for state in states[1:]:
        top = jnp.maximum(top, state[HS + 8 : HS + 9])
    total, mixed = 0.0, 0.0
    for state in states:
        factor = jnp.exp2((state[HS + 8 : HS + 9] - top) * LOG2)
        total = total + state[HS : HS + 1] * factor
        mixed = mixed + state[:HS] * factor
    return mixed, total, top


def merge_kernel(*refs):
    *refs, out_ref = refs
    tiles, _, rows = refs[-1].shape
    for tile in range(tiles):
        states = [ref[tile] for ref in refs]
        mixed, total, _ = combined([unspread(a) if a.dtype == jnp.bfloat16 else a for a in states])
        out_ref[tile * rows : (tile + 1) * rows, :] = jnp.transpose(mixed / total).astype(jnp.bfloat16)


def merge(name, *states, cost=1024):
    tiles, _, rows = states[-1].shape
    return pl.pallas_call(
        merge_kernel,
        name=name,
        out_shape=jax.ShapeDtypeStruct((tiles * rows, HS), jnp.bfloat16),
        cost_estimate=pl.CostEstimate(flops=cost, bytes_accessed=1024, transcendentals=0),
        compiler_params=pltpu.CompilerParams(vmem_limit_bytes=12 * 2**20),
    )(*states)


def spread(row):
    parts = []
    for _ in range(3):
        part = row.astype(jnp.bfloat16).astype(jnp.float32)
        parts.append(part)
        row = row - part
    return parts + [jnp.zeros((5, row.shape[1]), jnp.float32)]


def unspread(state):
    state = state.astype(jnp.float32)
    total = state[HS : HS + 1] + state[HS + 1 : HS + 2] + state[HS + 2 : HS + 3]
    top = state[HS + 8 : HS + 9] + state[HS + 9 : HS + 10] + state[HS + 10 : HS + 11]
    return jnp.concatenate([state[:HS], jnp.broadcast_to(total, (8, total.shape[1])), jnp.broadcast_to(top, (8, total.shape[1]))], axis=0)


def fold_kernel(own_ref, other_ref, *out_refs):
    tiles, _, rows = other_ref.shape
    width = out_refs[0].shape[2]
    each = rows // width
    for tile in range(tiles):
        mixed, total, top = combined([own_ref[tile], other_ref[tile]])
        for i in range(each):
            out = out_refs[tile * each + i]
            cut = slice(i * width, (i + 1) * width)
            rows_out = [mixed[:, cut]] + spread(total[:, cut]) + spread(top[:, cut])
            out[0] = jnp.concatenate(rows_out, axis=0).astype(jnp.bfloat16)


def fold(own, other, width):
    tiles, _, rows = other.shape
    return pl.pallas_call(
        fold_kernel,
        name="fold",
        out_shape=[jax.ShapeDtypeStruct((1, ROWS, width), jnp.bfloat16)] * (tiles * rows // width),
        cost_estimate=pl.CostEstimate(flops=1024, bytes_accessed=1024, transcendentals=0),
        compiler_params=pltpu.CompilerParams(vmem_limit_bytes=12 * 2**20),
    )(own, other)


def outgoing_kernel(*refs):
    *sources, out_ref, held, chunks, semaphores, leave = refs
    count = len(sources)
    token_rows = sources[0].shape[0]
    piece = token_rows // 4
    at = count * token_rows
    depth = token_rows // 3

    def arriving(i):
        cuts = [pl.ds(j * depth, depth) for j in range(3)]
        return [
            pltpu.make_async_copy(sources[i].at[cut], held.at[i, cut], semaphores.at[i, j]) for j, cut in enumerate(cuts)
        ]

    for i in range(count):
        for copy in arriving(i):
            copy.start()
    for i in range(count):
        for copy in arriving(i):
            copy.wait()
    leaving = []
    for target in range(16):
        z, yh, yl = target // 4, target // 2 % 2, target % 2
        head = 10 * yl + 2 * z + yh
        for i in range(count):
            chunks[target, i * token_rows : (i + 1) * token_rows, :] = held[i, :, head * HS : (head + 1) * HS]
        head = 10 * yl + 8 + yh
        pieces = [
            held[i, :, head * HS : (head + 1) * HS].astype(jnp.float32)[z * piece : (z + 1) * piece] for i in range(count)
        ]
        chunks[target, at:, :] = jnp.concatenate(pieces, axis=0).astype(jnp.bfloat16)
        leaving.append(pltpu.make_async_copy(chunks.at[target], out_ref.at[target], leave.at[target]))
        leaving[-1].start()
    for copy in leaving:
        copy.wait()


def outgoing(name, *arrays):
    rows = len(arrays) * arrays[0].shape[0] * 5 // 4
    return pl.pallas_call(
        outgoing_kernel,
        name=name,
        in_specs=[pl.BlockSpec(memory_space=pl.ANY)] * len(arrays),
        out_specs=pl.BlockSpec(memory_space=pl.ANY),
        out_shape=jax.ShapeDtypeStruct((16, rows, HS), jnp.bfloat16),
        scratch_shapes=[
            pltpu.VMEM((len(arrays), *arrays[0].shape), jnp.bfloat16),
            pltpu.VMEM((16, rows, HS), jnp.bfloat16),
            pltpu.SemaphoreType.DMA((len(arrays), 3)),
            pltpu.SemaphoreType.DMA((16,)),
        ],
        cost_estimate=pl.CostEstimate(flops=1024, bytes_accessed=1024, transcendentals=0),
        compiler_params=pltpu.CompilerParams(vmem_limit_bytes=60 * 2**20),
    )(*arrays)


def project_kernel(core_ref, att_ref, own_w, side_w, kept_ref, above_ref, below_ref, held, semaphores, *, start):
    core = core_ref[0]
    kept, half = kept_ref.shape[0], above_ref.shape[0]
    steps = kept_ref.shape[1] // WIDTH

    def columns(j, base=0):
        return pl.ds(pl.multiple_of(base + j * WIDTH, HS), WIDTH)

    def arriving(j):
        return pltpu.make_async_copy(side_w.at[:, columns(j, start)], held.at[j], semaphores.at[j])

    for j in range(steps):
        arriving(j).start()

    def group(number):
        return jnp.concatenate([att_ref[number * 5 + i] for i in range(5)], axis=1)

    own, side = group(core), group(1 - core)

    @pl.loop(0, steps)
    def _(j):
        total = jnp.dot(own, own_w[:, columns(j, start)], preferred_element_type=jnp.float32)
        arriving(j).wait()
        total = total + jnp.dot(side, held[j], preferred_element_type=jnp.float32)
        kept_ref[:, columns(j)] = total[:kept].astype(jnp.bfloat16)
        above_ref[:, columns(j)] = total[kept : kept + half].astype(jnp.bfloat16)
        below_ref[:, columns(j)] = total[kept + half :].astype(jnp.bfloat16)


def project(core, attended, own_w, side_w, start, columns):
    rows, steps = attended.shape[1], columns // WIDTH
    return pl.pallas_call(
        functools.partial(project_kernel, start=start),
        name="project",
        in_specs=[
            pl.BlockSpec(memory_space=pltpu.SMEM),
            pl.BlockSpec(memory_space=pltpu.VMEM),
            pl.BlockSpec(memory_space=pltpu.VMEM),
            pl.BlockSpec(memory_space=pl.ANY),
        ],
        out_shape=[
            jax.ShapeDtypeStruct((rows // 2, columns), jnp.bfloat16),
            jax.ShapeDtypeStruct((rows // 4, columns), jnp.bfloat16),
            jax.ShapeDtypeStruct((rows // 4, columns), jnp.bfloat16),
        ],
        scratch_shapes=[
            pltpu.VMEM((steps, side_w.shape[0], WIDTH), jnp.bfloat16),
            pltpu.SemaphoreType.DMA((steps,)),
        ],
        cost_estimate=pl.CostEstimate(flops=1024, bytes_accessed=1024, transcendentals=0),
        compiler_params=pltpu.CompilerParams(vmem_limit_bytes=24 * 2**20),
    )(core, attended, own_w, side_w)


def ring(array, axes, size, shift, name="ring"):
    with jax.named_scope(name):
        return lax.ppermute(array, axes, [(i, (i + shift) % size) for i in range(size)])


def cross(array, axis, bit, name):
    with jax.named_scope(name):
        return lax.ppermute(array, axis, [(i, i ^ bit) for i in range(4)])


def swap(array, name="swap"):
    with jax.named_scope(name):
        return lax.ppermute(array, "c", [(0, 1), (1, 0)])


def mask_tables(block_mask, frame_map):
    x, z, core = lax.axis_index("x"), lax.axis_index("z"), lax.axis_index("c")
    low, group = np.arange(2)[None, :, None], np.arange(3)
    at_core = np.arange(2)[:, None, None]
    ring_within = ((low * 2 + at_core) * 96 + group * 32) // BLOCK
    at_z = np.arange(4)[:, None, None, None]
    plane_within = ((low * 2 + at_core) * 96 + at_z * 24 + group * 8) // BLOCK

    def frames(at_x):
        return lax.dynamic_slice_in_dim(frame_map, at_x * 8, 8)[:, None, None] * FB

    def ring_blocks(at_x, at_core):
        within = jnp.asarray(ring_within.astype(np.int32))[at_core]
        return (frames(at_x) + within[None]).reshape(-1)

    def plane_blocks(at_x, at_core, at_z):
        within = jnp.asarray(plane_within.astype(np.int32))[at_z, at_core]
        return (frames(at_x) + within[None]).reshape(-1)

    ring_keys = jnp.concatenate([ring_blocks((x + i) % 4, core) for i in NEAR])
    plane_keys = jnp.concatenate([plane_blocks(x, core, z ^ i) for i in (0, 2, 1, 3)])
    blocks = jnp.arange(block_mask.shape[0], dtype=jnp.int32)
    pad = jnp.zeros((32,), jnp.int32)
    ring_queries, plane_queries = [], []
    for side in (0, 1):
        ring_queries += [ring_blocks(x, core ^ side), pad, pad, pad[:16]]
        for pair in (0, 2):
            plane_queries += [plane_blocks(x ^ (pair + i), core ^ side, z) for i in (0, 1)] + [pad]
    blocked = (block_mask <= 0).astype(jnp.bfloat16)

    def pick(index):
        return (index[:, None] == blocks[None, :]).astype(jnp.bfloat16)

    queries = pick(jnp.concatenate(ring_queries + plane_queries))
    by_query = jnp.dot(queries, blocked, preferred_element_type=jnp.float32).astype(jnp.bfloat16).reshape(6, HS, -1)

    def table(index, part):
        found = jnp.einsum("kb,tcb->tkc", pick(index), part, preferred_element_type=jnp.float32)
        return found * NEG

    return table(ring_keys, by_query[:2]), table(plane_keys, by_query[2:])


def local(queries, keys, values, w_out, block_mask, frame_map):
    core = lax.axis_index("c").astype(jnp.int32)
    z, low = lax.axis_index("z"), lax.axis_index("yl")
    token_rows = queries.shape[0]
    piece = token_rows // 4

    side_w = swap(w_out, "side_w")
    with jax.named_scope("spread"):
        sent = lax.all_to_all(outgoing("outgoing", keys, values, queries), RING, 0, 0)
    one, two, three = token_rows, 2 * token_rows, 3 * token_rows
    ring_kv = jnp.concatenate([sent[:, :one], sent[:, one:two]], axis=0).reshape(-1, HS)
    ring_q = sent[:, two:three].reshape(-1, HS)
    plane_kv = jnp.concatenate([sent[:, three : three + piece], sent[:, three + piece : three + 2 * piece]], axis=0)
    plane_kv = plane_kv.reshape(-1, HS)
    plane_q = sent[:, three + 2 * piece :].reshape(-1, HS)
    ring_rows = 16 * token_rows
    plane_rows = 16 * piece

    ring_masks, plane_masks = mask_tables(block_mask, frame_map)

    side_w, ring_kv, ring_q, plane_kv, plane_q = lax.optimization_barrier((side_w, ring_kv, ring_q, plane_kv, plane_q))
    ring_left, ring_right = ring(ring_kv, "x", 4, 1, "ring_x"), ring(ring_kv, "x", 4, -1, "ring_x")
    query_a = jnp.stack([ring_q, swap(ring_q, "swap_q")])

    plane_kv = [plane_kv] + [cross(plane_kv, "z", i, "plane_z") for i in (2, 1, 3)]
    plane_q = jnp.concatenate([plane_q] + [cross(plane_q, "x", i, "plane_q") for i in (1, 2, 3)], axis=0)
    query_b = jnp.concatenate([plane_q, swap(plane_q, "swap_plane_q")], axis=0).reshape(4, 2 * plane_rows, HS)
    query_a, query_b = lax.optimization_barrier((query_a, query_b))
    whole = [(0, 0, 0, ring_rows, ring_rows)]
    state = attention("own", query_a, ring_masks[:, :48], 32, [ring_kv], whole)
    plane_parts = [(i, 0, i, plane_rows, plane_rows) for i in range(4)]
    query_b, state = lax.optimization_barrier((query_b, state))
    plane_state = attention("plane", query_b, plane_masks, 8, plane_kv, plane_parts, small=128)

    plane_state, state, ring_left, ring_right = lax.optimization_barrier((plane_state, state, ring_left, ring_right))
    other_b = swap(plane_state[0][2:], "swap_b")
    middle = ring_kv.shape[0] // 2
    ring_far = [
        ring(ring_left[:middle], "x", 4, 1, "ring_x_far"),
        ring(ring_right[middle:], "x", 4, -1, "ring_x_far"),
    ]
    state = attention("left", query_a, ring_masks[:, 48:96], 32, [ring_left], whole, state)
    own_part, other_b, state = lax.optimization_barrier((plane_state[0], other_b, state))
    plane_part = fold(own_part, other_b, plane_rows)
    plane_part, state = lax.optimization_barrier((plane_part, state))
    plane_part = [plane_part[0]] + [cross(plane_part[i], "x", i, "plane_sum") for i in (1, 2, 3)]
    state = attention("right", query_a, ring_masks[:, 96:144], 32, [ring_right], whole, state)
    out_b = merge("merge_plane", *plane_part).reshape(4, 2, 2, piece, HS)
    out_b, state = lax.optimization_barrier((out_b, state))
    far = [(0, 0, 1, 0, ring_rows)]
    far_masks = ring_masks[:, 144:]
    side = attention("far_side", query_a, far_masks, 32, ring_far, far, state, skip=1, tiles=1)
    other_a = swap(side[0], "swap_a")
    state, side = lax.optimization_barrier((state, side))
    own = attention("far_own", query_a, far_masks, 32, ring_far, far, state, skip=0, tiles=1)
    out_a = merge("merge_ring", own[0], other_a, cost=1 << 32).reshape(4, 2, 2, token_rows, HS)

    def split(array):
        first, second = array[:, :, 0], array[:, :, 1]
        same = jnp.where(low == 0, first, second)
        other = jnp.where(low == 0, second, first)
        flipped = jnp.stack([other[:, 1], other[:, 0]], axis=1)
        below = jnp.where(low == 0, flipped, other)
        above = jnp.where(low == 0, other, flipped)
        return same, below, above

    half = token_rows // 2
    same, below, above = split(out_a)
    piece_same, piece_below, piece_above = split(out_b)
    back = jnp.concatenate(
        [same, below[:, :, :half], above[:, :, half:], piece_same, jnp.where(z < 2, piece_below, piece_above)], axis=2
    ).reshape(8, -1, HS)
    with jax.named_scope("return"):
        back = lax.all_to_all(back, ("z", "yh"), 0, 0)
    rows = 2 * token_rows
    plane_back = back[:, rows:].reshape(4, 2, 2, piece, HS).transpose(1, 2, 0, 3, 4).reshape(2, rows, HS)
    attended = jnp.concatenate([back[:, :rows], plane_back], axis=0)

    outs = []
    columns = w_out.shape[1] // CHUNKS
    for i in range(CHUNKS):
        kept, to_below, to_above = project(core[None], attended, w_out, side_w, i * columns, columns)
        from_above, from_below = ring(to_below, Y, 4, -1, "sum_y"), ring(to_above, Y, 4, 1, "sum_y")
        other = jnp.concatenate([from_above, from_below], axis=0)
        out = (kept.astype(jnp.float32) + other.astype(jnp.float32)).astype(jnp.bfloat16)
        outs.append(out if i == CHUNKS - 1 else lax.optimization_barrier(out))
    return outs[0] if CHUNKS == 1 else jnp.concatenate(outs, axis=1)


def solution(mesh):
    fine = jax.sharding.Mesh(mesh.devices.reshape(4, 4, 2, 2, 2), ALL)
    rows = P(ALL, None)
    placed = (rows, rows, rows, P(("yl", "c"), None), P(), P())
    return jax.shard_map(local, mesh=fine, in_specs=placed, out_specs=rows, check_vma=False)
```

```python
import functools

import jax
import jax.numpy as jnp
import numpy as np
from jax import lax
from jax.experimental import pallas as pl
from jax.experimental.pallas import tpu as pltpu
from jax.sharding import PartitionSpec as P

HS = 128
BLOCK = 64
FRAME = 384
FB = FRAME // BLOCK
NEG = -1e30
SCALE = HS ** -0.5
LOG2 = float(SCALE * np.log2(np.e))
BOUND = 60.0

RING = ("z", "yh", "yl")
Y = ("yh", "yl")
ALL = ("x", "z", "yh", "yl", "c")
WIDTH = 1280
CHUNKS = 2
NEAR = (0, 3, 1, 2)
ROWS = 144


def square_norm_max(rows):
    wide = rows.astype(jnp.float32)
    return jnp.max(jnp.sum(wide * wide, axis=1, keepdims=True))


def attention_kernel(*refs, first, count, parts, sub, small, skip):
    q_ref, mt_ref = refs[0], refs[1]
    sources = refs[2 : 2 + count]
    if first:
        state_in = norm_in = None
        state_out, norm_out = refs[2 + count :]
    else:
        norm_in, state_in, state_out, norm_out = refs[2 + count :]
    _, rows, _ = q_ref.shape

    def joined(slices):
        return slices[0] if len(slices) == 1 else jnp.concatenate(slices, axis=0)

    def with_masks(key, tile, mask_at, size):
        masks = mt_ref[tile, pl.ds(mask_at, size // sub), :]
        masks = jnp.broadcast_to(masks[:, None, :], (size // sub, sub, HS)).reshape(size, HS)
        return jnp.concatenate([key, masks.astype(jnp.bfloat16)], axis=1)

    def scores(key, query):
        return lax.dot_general(key, query, (((1,), (1,)), ((), ())), preferred_element_type=jnp.float32)

    def mixed(value, weights):
        return lax.dot_general(
            value, weights.astype(jnp.bfloat16), (((0,), (0,)), ((), ())), preferred_element_type=jnp.float32
        )

    all_keys = sum(part[4] for part in parts)

    @pl.loop(0, state_out.shape[0])
    def _(at_tile):
        tile = at_tile + skip
        place = lax.broadcasted_iota(jnp.int32, (rows, HS), 0) // sub
        one_hot = jnp.where(place == lax.broadcasted_iota(jnp.int32, (rows, HS), 1), 1.0, 0.0).astype(jnp.bfloat16)
        query = jnp.concatenate([q_ref[tile], one_hot], axis=1)
        key = joined([sources[k][at : at + keys, :] for k, at, _, _, keys in parts])
        value = joined([sources[v][at : at + keys, :] for _, _, v, at, keys in parts])
        weights = jnp.exp2(scores(with_masks(key, tile, 0, all_keys), query) * LOG2)
        total = jnp.sum(weights, axis=0, keepdims=True)
        weighted = mixed(value, weights)
        if not first:
            total = state_in[tile, HS : HS + 1, :] + total
            weighted = state_in[tile, :HS, :] + weighted
        state_out[at_tile, :HS, :] = weighted
        state_out[at_tile, HS : HS + 8, :] = jnp.broadcast_to(total, (8, rows))
        state_out[at_tile, HS + 8 :, :] = jnp.broadcast_to(jnp.where(total > 0.0, 0.0, NEG), (8, rows))

        query_norm = square_norm_max(q_ref[tile]) if first else jnp.max(norm_in[tile])
        bounded = jnp.logical_and(query_norm >= 0.0, query_norm * square_norm_max(key) <= (BOUND / SCALE) ** 2)
        norm_out[at_tile] = jnp.full((8, HS), jnp.where(bounded, query_norm, -1.0), jnp.float32)

        @pl.when(jnp.logical_not(bounded))
        def _():
            if first:
                state_out[at_tile, : HS + 8, :] = jnp.zeros((HS + 8, rows), jnp.float32)
                state_out[at_tile, HS + 8 :, :] = jnp.full((8, rows), NEG, jnp.float32)
            else:
                state_out[at_tile] = state_in[tile]
            mask_base = 0
            for k_source, k_at, v_source, v_at, keys in parts:

                @pl.loop(0, keys // small)
                def _(j):
                    key = sources[k_source][pl.ds(pl.multiple_of(k_at + j * small, small), small), :]
                    value = sources[v_source][pl.ds(pl.multiple_of(v_at + j * small, small), small), :]
                    mask_at = pl.multiple_of(mask_base + j * (small // sub), 8)
                    found = scores(with_masks(key, tile, mask_at, small), query)
                    top = state_out[at_tile, HS + 8 : HS + 9, :]
                    new_top = jnp.maximum(top, jnp.max(found, axis=0, keepdims=True))
                    factor = jnp.exp2((top - new_top) * LOG2)
                    weights = jnp.exp2((found - new_top) * LOG2)
                    total = state_out[at_tile, HS : HS + 1, :] * factor + jnp.sum(weights, axis=0, keepdims=True)
                    state_out[at_tile, HS : HS + 8, :] = jnp.broadcast_to(total, (8, rows))
                    state_out[at_tile, :HS, :] = state_out[at_tile, :HS, :] * factor + mixed(value, weights)
                    state_out[at_tile, HS + 8 :, :] = jnp.broadcast_to(new_top, (8, rows))

                mask_base += keys // sub


def attention(name, query, masks, sub, sources, parts, state=None, small=256, skip=0, tiles=None, cost=1024):
    rows = query.shape[1]
    first = state is None
    tiles = query.shape[0] if tiles is None else tiles
    operands = [query, masks, *sources]
    if not first:
        operands += [state[1], state[0]]
    return pl.pallas_call(
        functools.partial(
            attention_kernel, first=first, count=len(sources), parts=tuple(parts), sub=sub, small=small, skip=skip
        ),
        out_shape=[
            jax.ShapeDtypeStruct((tiles, ROWS, rows), jnp.float32),
            jax.ShapeDtypeStruct((tiles, 8, HS), jnp.float32),
        ],
        cost_estimate=pl.CostEstimate(flops=cost, bytes_accessed=1024, transcendentals=0),
        compiler_params=pltpu.CompilerParams(vmem_limit_bytes=20 * 2**20),
        name=name,
    )(*operands)


def combined(states):
    top = states[0][HS + 8 : HS + 9]
    for state in states[1:]:
        top = jnp.maximum(top, state[HS + 8 : HS + 9])
    total, mixed = 0.0, 0.0
    for state in states:
        factor = jnp.exp2((state[HS + 8 : HS + 9] - top) * LOG2)
        total = total + state[HS : HS + 1] * factor
        mixed = mixed + state[:HS] * factor
    return mixed, total, top


def merge_kernel(*refs):
    *refs, out_ref = refs
    tiles, _, rows = refs[-1].shape
    for tile in range(tiles):
        states = [ref[tile] for ref in refs]
        mixed, total, _ = combined([unspread(a) if a.dtype == jnp.bfloat16 else a for a in states])
        out_ref[tile * rows : (tile + 1) * rows, :] = jnp.transpose(mixed / total).astype(jnp.bfloat16)


def merge(name, *states, cost=1024):
    tiles, _, rows = states[-1].shape
    return pl.pallas_call(
        merge_kernel,
        name=name,
        out_shape=jax.ShapeDtypeStruct((tiles * rows, HS), jnp.bfloat16),
        cost_estimate=pl.CostEstimate(flops=cost, bytes_accessed=1024, transcendentals=0),
        compiler_params=pltpu.CompilerParams(vmem_limit_bytes=12 * 2**20),
    )(*states)


def spread(row):
    parts = []
    for _ in range(3):
        part = row.astype(jnp.bfloat16).astype(jnp.float32)
        parts.append(part)
        row = row - part
    return parts + [jnp.zeros((5, row.shape[1]), jnp.float32)]


def unspread(state):
    state = state.astype(jnp.float32)
    total = state[HS : HS + 1] + state[HS + 1 : HS + 2] + state[HS + 2 : HS + 3]
    top = state[HS + 8 : HS + 9] + state[HS + 9 : HS + 10] + state[HS + 10 : HS + 11]
    return jnp.concatenate([state[:HS], jnp.broadcast_to(total, (8, total.shape[1])), jnp.broadcast_to(top, (8, total.shape[1]))], axis=0)


def fold_kernel(own_ref, other_ref, *out_refs):
    tiles, _, rows = other_ref.shape
    width = out_refs[0].shape[2]
    each = rows // width
    for tile in range(tiles):
        mixed, total, top = combined([own_ref[tile], other_ref[tile]])
        for i in range(each):
            out = out_refs[tile * each + i]
            cut = slice(i * width, (i + 1) * width)
            rows_out = [mixed[:, cut]] + spread(total[:, cut]) + spread(top[:, cut])
            out[0] = jnp.concatenate(rows_out, axis=0).astype(jnp.bfloat16)


def fold(own, other, width):
    tiles, _, rows = other.shape
    return pl.pallas_call(
        fold_kernel,
        name="fold",
        out_shape=[jax.ShapeDtypeStruct((1, ROWS, width), jnp.bfloat16)] * (tiles * rows // width),
        cost_estimate=pl.CostEstimate(flops=1024, bytes_accessed=1024, transcendentals=0),
        compiler_params=pltpu.CompilerParams(vmem_limit_bytes=12 * 2**20),
    )(own, other)


def outgoing_kernel(*refs):
    *sources, out_ref, held, chunks, semaphores, leave = refs
    count = len(sources)
    token_rows = sources[0].shape[0]
    piece = token_rows // 4
    at = count * token_rows
    depth = token_rows // 3

    def arriving(i):
        cuts = [pl.ds(j * depth, depth) for j in range(3)]
        return [
            pltpu.make_async_copy(sources[i].at[cut], held.at[i, cut], semaphores.at[i, j]) for j, cut in enumerate(cuts)
        ]

    for i in range(count):
        for copy in arriving(i):
            copy.start()
    for i in range(count):
        for copy in arriving(i):
            copy.wait()
    leaving = []
    for target in range(16):
        z, yh, yl = target // 4, target // 2 % 2, target % 2
        head = 10 * yl + 2 * z + yh
        for i in range(count):
            chunks[target, i * token_rows : (i + 1) * token_rows, :] = held[i, :, head * HS : (head + 1) * HS]
        head = 10 * yl + 8 + yh
        pieces = [
            held[i, :, head * HS : (head + 1) * HS].astype(jnp.float32)[z * piece : (z + 1) * piece] for i in range(count)
        ]
        pieces.append(jnp.zeros((chunks.shape[1] - at - count * piece, HS), jnp.float32))
        chunks[target, at:, :] = jnp.concatenate(pieces, axis=0).astype(jnp.bfloat16)
        leaving.append(pltpu.make_async_copy(chunks.at[target], out_ref.at[target], leave.at[target]))
        leaving[-1].start()
    for copy in leaving:
        copy.wait()


def outgoing(name, *arrays):
    rows = len(arrays) * arrays[0].shape[0] * 5 // 4
    rows += -rows % 16
    return pl.pallas_call(
        outgoing_kernel,
        name=name,
        in_specs=[pl.BlockSpec(memory_space=pl.ANY)] * len(arrays),
        out_specs=pl.BlockSpec(memory_space=pl.ANY),
        out_shape=jax.ShapeDtypeStruct((16, rows, HS), jnp.bfloat16),
        scratch_shapes=[
            pltpu.VMEM((len(arrays), *arrays[0].shape), jnp.bfloat16),
            pltpu.VMEM((16, rows, HS), jnp.bfloat16),
            pltpu.SemaphoreType.DMA((len(arrays), 3)),
            pltpu.SemaphoreType.DMA((16,)),
        ],
        cost_estimate=pl.CostEstimate(flops=1024, bytes_accessed=1024, transcendentals=0),
        compiler_params=pltpu.CompilerParams(vmem_limit_bytes=60 * 2**20),
    )(*arrays)


def project_kernel(core_ref, att_ref, own_w, side_w, kept_ref, above_ref, below_ref, held, semaphores, *, start):
    core = core_ref[0]
    kept, half = kept_ref.shape[0], above_ref.shape[0]
    steps = kept_ref.shape[1] // WIDTH

    def columns(j, base=0):
        return pl.ds(pl.multiple_of(base + j * WIDTH, HS), WIDTH)

    def arriving(j):
        return pltpu.make_async_copy(side_w.at[:, columns(j, start)], held.at[j], semaphores.at[j])

    for j in range(steps):
        arriving(j).start()

    def group(number):
        return jnp.concatenate([att_ref[number * 5 + i] for i in range(5)], axis=1)

    own, side = group(core), group(1 - core)

    @pl.loop(0, steps)
    def _(j):
        total = jnp.dot(own, own_w[:, columns(j, start)], preferred_element_type=jnp.float32)
        arriving(j).wait()
        total = total + jnp.dot(side, held[j], preferred_element_type=jnp.float32)
        kept_ref[:, columns(j)] = total[:kept].astype(jnp.bfloat16)
        above_ref[:, columns(j)] = total[kept : kept + half].astype(jnp.bfloat16)
        below_ref[:, columns(j)] = total[kept + half :].astype(jnp.bfloat16)


def project(core, attended, own_w, side_w, start, columns):
    rows, steps = attended.shape[1], columns // WIDTH
    return pl.pallas_call(
        functools.partial(project_kernel, start=start),
        name="project",
        in_specs=[
            pl.BlockSpec(memory_space=pltpu.SMEM),
            pl.BlockSpec(memory_space=pltpu.VMEM),
            pl.BlockSpec(memory_space=pltpu.VMEM),
            pl.BlockSpec(memory_space=pl.ANY),
        ],
        out_shape=[
            jax.ShapeDtypeStruct((rows // 2, columns), jnp.bfloat16),
            jax.ShapeDtypeStruct((rows // 4, columns), jnp.bfloat16),
            jax.ShapeDtypeStruct((rows // 4, columns), jnp.bfloat16),
        ],
        scratch_shapes=[
            pltpu.VMEM((steps, side_w.shape[0], WIDTH), jnp.bfloat16),
            pltpu.SemaphoreType.DMA((steps,)),
        ],
        cost_estimate=pl.CostEstimate(flops=1024, bytes_accessed=1024, transcendentals=0),
        compiler_params=pltpu.CompilerParams(vmem_limit_bytes=24 * 2**20),
    )(core, attended, own_w, side_w)


def ring(array, axes, size, shift, name="ring"):
    with jax.named_scope(name):
        return lax.ppermute(array, axes, [(i, (i + shift) % size) for i in range(size)])


def cross(array, axis, bit, name):
    with jax.named_scope(name):
        return lax.ppermute(array, axis, [(i, i ^ bit) for i in range(4)])


def swap(array, name="swap"):
    with jax.named_scope(name):
        return lax.ppermute(array, "c", [(0, 1), (1, 0)])


def mask_tables(block_mask, frame_map):
    x, z, core = lax.axis_index("x"), lax.axis_index("z"), lax.axis_index("c")
    low, group = np.arange(2)[None, :, None], np.arange(3)
    at_core = np.arange(2)[:, None, None]
    ring_within = ((low * 2 + at_core) * 96 + group * 32) // BLOCK
    at_z = np.arange(4)[:, None, None, None]
    plane_within = ((low * 2 + at_core) * 96 + at_z * 24 + group * 8) // BLOCK

    def frames(at_x):
        return lax.dynamic_slice_in_dim(frame_map, at_x * 8, 8)[:, None, None] * FB

    def ring_blocks(at_x, at_core):
        within = jnp.asarray(ring_within.astype(np.int32))[at_core]
        return (frames(at_x) + within[None]).reshape(-1)

    def plane_blocks(at_x, at_core, at_z):
        within = jnp.asarray(plane_within.astype(np.int32))[at_z, at_core]
        return (frames(at_x) + within[None]).reshape(-1)

    ring_keys = jnp.concatenate([ring_blocks((x + i) % 4, core) for i in NEAR])
    plane_keys = jnp.concatenate([plane_blocks(x, core, z ^ i) for i in (0, 2, 1, 3)])
    blocks = jnp.arange(block_mask.shape[0], dtype=jnp.int32)
    pad = jnp.zeros((32,), jnp.int32)
    ring_queries, plane_queries = [], []
    for side in (0, 1):
        ring_queries += [ring_blocks(x, core ^ side), pad, pad, pad[:16]]
        for pair in (0, 2):
            plane_queries += [plane_blocks(x ^ (pair + i), core ^ side, z) for i in (0, 1)] + [pad]
    blocked = (block_mask <= 0).astype(jnp.bfloat16)

    def pick(index):
        return (index[:, None] == blocks[None, :]).astype(jnp.bfloat16)

    queries = pick(jnp.concatenate(ring_queries + plane_queries))
    by_query = jnp.dot(queries, blocked, preferred_element_type=jnp.float32).astype(jnp.bfloat16).reshape(6, HS, -1)

    def table(index, part):
        found = jnp.einsum("kb,tcb->tkc", pick(index), part, preferred_element_type=jnp.float32)
        return found * NEG

    return table(ring_keys, by_query[:2]), table(plane_keys, by_query[2:])


def local(queries, keys, values, w_out, block_mask, frame_map):
    core = lax.axis_index("c").astype(jnp.int32)
    z, low = lax.axis_index("z"), lax.axis_index("yl")
    token_rows = queries.shape[0]
    piece = token_rows // 4

    side_w = swap(w_out, "side_w")
    with jax.named_scope("spread"):
        sent = lax.all_to_all(outgoing("outgoing", keys, values, queries), RING, 0, 0)
    one, two, three = token_rows, 2 * token_rows, 3 * token_rows
    ring_kv = jnp.concatenate([sent[:, :one], sent[:, one:two]], axis=0).reshape(-1, HS)
    ring_q = sent[:, two:three].reshape(-1, HS)
    plane_kv = jnp.concatenate([sent[:, three : three + piece], sent[:, three + piece : three + 2 * piece]], axis=0)
    plane_kv = plane_kv.reshape(-1, HS)
    plane_q = sent[:, three + 2 * piece : three + 3 * piece].reshape(-1, HS)
    ring_rows = 16 * token_rows
    plane_rows = 16 * piece

    ring_masks, plane_masks = mask_tables(block_mask, frame_map)

    side_w, ring_kv, ring_q, plane_kv, plane_q = lax.optimization_barrier((side_w, ring_kv, ring_q, plane_kv, plane_q))
    ring_left, ring_right = ring(ring_kv, "x", 4, 1, "ring_x"), ring(ring_kv, "x", 4, -1, "ring_x")
    query_a = jnp.stack([ring_q, swap(ring_q, "swap_q")])

    plane_kv = [plane_kv] + [cross(plane_kv, "z", i, "plane_z") for i in (2, 1, 3)]
    plane_q = jnp.concatenate([plane_q] + [cross(plane_q, "x", i, "plane_q") for i in (1, 2, 3)], axis=0)
    query_b = jnp.concatenate([plane_q, swap(plane_q, "swap_plane_q")], axis=0).reshape(4, 2 * plane_rows, HS)
    query_a, query_b = lax.optimization_barrier((query_a, query_b))
    whole = [(0, 0, 0, ring_rows, ring_rows)]
    state = attention("own", query_a, ring_masks[:, :48], 32, [ring_kv], whole)
    plane_parts = [(i, 0, i, plane_rows, plane_rows) for i in range(4)]
    query_b, state = lax.optimization_barrier((query_b, state))
    plane_state = attention("plane", query_b, plane_masks, 8, plane_kv, plane_parts, small=128)

    plane_state, state, ring_left, ring_right = lax.optimization_barrier((plane_state, state, ring_left, ring_right))
    other_b = swap(plane_state[0][2:], "swap_b")
    middle = ring_kv.shape[0] // 2
    ring_far = [
        ring(ring_left[:middle], "x", 4, 1, "ring_x_far"),
        ring(ring_right[middle:], "x", 4, -1, "ring_x_far"),
    ]
    plane_part = fold(plane_state[0], other_b, plane_rows)
    plane_part, state = lax.optimization_barrier((plane_part, state))
    plane_part = [plane_part[0]] + [cross(plane_part[i], "x", i, "plane_sum") for i in (1, 2, 3)]
    state = attention("left", query_a, ring_masks[:, 48:96], 32, [ring_left], whole, state)
    state = attention("right", query_a, ring_masks[:, 96:144], 32, [ring_right], whole, state)
    out_b = merge("merge_plane", *plane_part).reshape(4, 2, 2, piece, HS)
    out_b, state = lax.optimization_barrier((out_b, state))
    far = [(0, 0, 1, 0, ring_rows)]
    far_masks = ring_masks[:, 144:]
    side = attention("far_side", query_a, far_masks, 32, ring_far, far, state, skip=1, tiles=1)
    other_a = swap(side[0], "swap_a")
    state, side = lax.optimization_barrier((state, side))
    own = attention("far_own", query_a, far_masks, 32, ring_far, far, state, skip=0, tiles=1)
    out_a = merge("merge_ring", own[0], other_a, cost=1 << 32).reshape(4, 2, 2, token_rows, HS)

    def split(array):
        first, second = array[:, :, 0], array[:, :, 1]
        same = jnp.where(low == 0, first, second)
        other = jnp.where(low == 0, second, first)
        flipped = jnp.stack([other[:, 1], other[:, 0]], axis=1)
        below = jnp.where(low == 0, flipped, other)
        above = jnp.where(low == 0, other, flipped)
        return same, below, above

    half = token_rows // 2
    same, below, above = split(out_a)
    piece_same, piece_below, piece_above = split(out_b)
    back = jnp.concatenate(
        [same, below[:, :, :half], above[:, :, half:], piece_same, jnp.where(z < 2, piece_below, piece_above)], axis=2
    ).reshape(8, -1, HS)
    with jax.named_scope("return"):
        back = lax.all_to_all(back, ("z", "yh"), 0, 0)
    rows = 2 * token_rows
    plane_back = back[:, rows:].reshape(4, 2, 2, piece, HS).transpose(1, 2, 0, 3, 4).reshape(2, rows, HS)
    attended = jnp.concatenate([back[:, :rows], plane_back], axis=0)

    outs = []
    columns = w_out.shape[1] // CHUNKS
    for i in range(CHUNKS):
        kept, to_below, to_above = project(core[None], attended, w_out, side_w, i * columns, columns)
        from_above, from_below = ring(to_below, Y, 4, -1, "sum_y"), ring(to_above, Y, 4, 1, "sum_y")
        other = jnp.concatenate([from_above, from_below], axis=0)
        out = (kept.astype(jnp.float32) + other.astype(jnp.float32)).astype(jnp.bfloat16)
        outs.append(out if i == CHUNKS - 1 else lax.optimization_barrier(out))
    return outs[0] if CHUNKS == 1 else jnp.concatenate(outs, axis=1)


def solution(mesh):
    fine = jax.sharding.Mesh(mesh.devices.reshape(4, 4, 2, 2, 2), ALL)
    rows = P(ALL, None)
    placed = (rows, rows, rows, P(("yl", "c"), None), P(), P())
    return jax.shard_map(local, mesh=fine, in_specs=placed, out_specs=rows, check_vma=False)
```

```python
import functools

import jax
import jax.numpy as jnp
import numpy as np
from jax import lax
from jax.experimental import pallas as pl
from jax.experimental.pallas import tpu as pltpu
from jax.sharding import PartitionSpec as P

HS = 128
BLOCK = 64
FRAME = 384
FB = FRAME // BLOCK
NEG = -1e30
SCALE = HS ** -0.5
LOG2 = float(SCALE * np.log2(np.e))
BOUND = 60.0

RING = ("z", "yh", "yl")
Y = ("yh", "yl")
ALL = ("x", "z", "yh", "yl", "c")
WIDTH = 1280
CHUNKS = 2
NEAR = (0, 3, 1, 2)
ROWS = 144


def square_norm_max(rows):
    wide = rows.astype(jnp.float32)
    return jnp.max(jnp.sum(wide * wide, axis=1, keepdims=True))


def attention_kernel(*refs, first, count, parts, sub, small, skip):
    q_ref, mt_ref = refs[0], refs[1]
    sources = refs[2 : 2 + count]
    if first:
        state_in = norm_in = None
        state_out, norm_out = refs[2 + count :]
    else:
        norm_in, state_in, state_out, norm_out = refs[2 + count :]
    _, rows, _ = q_ref.shape

    def joined(slices):
        return slices[0] if len(slices) == 1 else jnp.concatenate(slices, axis=0)

    def with_masks(key, tile, mask_at, size):
        masks = mt_ref[tile, pl.ds(mask_at, size // sub), :]
        masks = jnp.broadcast_to(masks[:, None, :], (size // sub, sub, HS)).reshape(size, HS)
        return jnp.concatenate([key, masks.astype(jnp.bfloat16)], axis=1)

    def scores(key, query):
        return lax.dot_general(key, query, (((1,), (1,)), ((), ())), preferred_element_type=jnp.float32)

    def mixed(value, weights):
        return lax.dot_general(
            value, weights.astype(jnp.bfloat16), (((0,), (0,)), ((), ())), preferred_element_type=jnp.float32
        )

    all_keys = sum(part[4] for part in parts)

    @pl.loop(0, state_out.shape[0])
    def _(at_tile):
        tile = at_tile + skip
        place = lax.broadcasted_iota(jnp.int32, (rows, HS), 0) // sub
        one_hot = jnp.where(place == lax.broadcasted_iota(jnp.int32, (rows, HS), 1), 1.0, 0.0).astype(jnp.bfloat16)
        query = jnp.concatenate([q_ref[tile], one_hot], axis=1)
        key = joined([sources[k][at : at + keys, :] for k, at, _, _, keys in parts])
        value = joined([sources[v][at : at + keys, :] for _, _, v, at, keys in parts])
        weights = jnp.exp2(scores(with_masks(key, tile, 0, all_keys), query) * LOG2)
        total = jnp.sum(weights, axis=0, keepdims=True)
        weighted = mixed(value, weights)
        if not first:
            total = state_in[tile, HS : HS + 1, :] + total
            weighted = state_in[tile, :HS, :] + weighted
        state_out[at_tile, :HS, :] = weighted
        state_out[at_tile, HS : HS + 8, :] = jnp.broadcast_to(total, (8, rows))
        state_out[at_tile, HS + 8 :, :] = jnp.broadcast_to(jnp.where(total > 0.0, 0.0, NEG), (8, rows))

        query_norm = square_norm_max(q_ref[tile]) if first else jnp.max(norm_in[tile])
        bounded = jnp.logical_and(query_norm >= 0.0, query_norm * square_norm_max(key) <= (BOUND / SCALE) ** 2)
        norm_out[at_tile] = jnp.full((8, HS), jnp.where(bounded, query_norm, -1.0), jnp.float32)

        @pl.when(jnp.logical_not(bounded))
        def _():
            if first:
                state_out[at_tile, : HS + 8, :] = jnp.zeros((HS + 8, rows), jnp.float32)
                state_out[at_tile, HS + 8 :, :] = jnp.full((8, rows), NEG, jnp.float32)
            else:
                state_out[at_tile] = state_in[tile]
            mask_base = 0
            for k_source, k_at, v_source, v_at, keys in parts:

                @pl.loop(0, keys // small)
                def _(j):
                    key = sources[k_source][pl.ds(pl.multiple_of(k_at + j * small, small), small), :]
                    value = sources[v_source][pl.ds(pl.multiple_of(v_at + j * small, small), small), :]
                    mask_at = pl.multiple_of(mask_base + j * (small // sub), 8)
                    found = scores(with_masks(key, tile, mask_at, small), query)
                    top = state_out[at_tile, HS + 8 : HS + 9, :]
                    new_top = jnp.maximum(top, jnp.max(found, axis=0, keepdims=True))
                    factor = jnp.exp2((top - new_top) * LOG2)
                    weights = jnp.exp2((found - new_top) * LOG2)
                    total = state_out[at_tile, HS : HS + 1, :] * factor + jnp.sum(weights, axis=0, keepdims=True)
                    state_out[at_tile, HS : HS + 8, :] = jnp.broadcast_to(total, (8, rows))
                    state_out[at_tile, :HS, :] = state_out[at_tile, :HS, :] * factor + mixed(value, weights)
                    state_out[at_tile, HS + 8 :, :] = jnp.broadcast_to(new_top, (8, rows))

                mask_base += keys // sub


def attention(name, query, masks, sub, sources, parts, state=None, small=256, skip=0, tiles=None, cost=1024):
    rows = query.shape[1]
    first = state is None
    tiles = query.shape[0] if tiles is None else tiles
    operands = [query, masks, *sources]
    if not first:
        operands += [state[1], state[0]]
    return pl.pallas_call(
        functools.partial(
            attention_kernel, first=first, count=len(sources), parts=tuple(parts), sub=sub, small=small, skip=skip
        ),
        out_shape=[
            jax.ShapeDtypeStruct((tiles, ROWS, rows), jnp.float32),
            jax.ShapeDtypeStruct((tiles, 8, HS), jnp.float32),
        ],
        cost_estimate=pl.CostEstimate(flops=cost, bytes_accessed=1024, transcendentals=0),
        compiler_params=pltpu.CompilerParams(vmem_limit_bytes=20 * 2**20),
        name=name,
    )(*operands)


def combined(states):
    top = states[0][HS + 8 : HS + 9]
    for state in states[1:]:
        top = jnp.maximum(top, state[HS + 8 : HS + 9])
    total, mixed = 0.0, 0.0
    for state in states:
        factor = jnp.exp2((state[HS + 8 : HS + 9] - top) * LOG2)
        total = total + state[HS : HS + 1] * factor
        mixed = mixed + state[:HS] * factor
    return mixed, total, top


def merge_kernel(*refs):
    *refs, out_ref = refs
    tiles, _, rows = refs[-1].shape
    for tile in range(tiles):
        states = [ref[tile] for ref in refs]
        mixed, total, _ = combined([unspread(a) if a.dtype == jnp.bfloat16 else a for a in states])
        out_ref[tile * rows : (tile + 1) * rows, :] = jnp.transpose(mixed / total).astype(jnp.bfloat16)


def merge(name, *states, cost=1024):
    tiles, _, rows = states[-1].shape
    return pl.pallas_call(
        merge_kernel,
        name=name,
        out_shape=jax.ShapeDtypeStruct((tiles * rows, HS), jnp.bfloat16),
        cost_estimate=pl.CostEstimate(flops=cost, bytes_accessed=1024, transcendentals=0),
        compiler_params=pltpu.CompilerParams(vmem_limit_bytes=12 * 2**20),
    )(*states)


def spread(row):
    parts = []
    for _ in range(3):
        part = row.astype(jnp.bfloat16).astype(jnp.float32)
        parts.append(part)
        row = row - part
    return parts + [jnp.zeros((5, row.shape[1]), jnp.float32)]


def unspread(state):
    state = state.astype(jnp.float32)
    total = state[HS : HS + 1] + state[HS + 1 : HS + 2] + state[HS + 2 : HS + 3]
    top = state[HS + 8 : HS + 9] + state[HS + 9 : HS + 10] + state[HS + 10 : HS + 11]
    return jnp.concatenate([state[:HS], jnp.broadcast_to(total, (8, total.shape[1])), jnp.broadcast_to(top, (8, total.shape[1]))], axis=0)


def fold_kernel(own_ref, other_ref, *out_refs):
    tiles, _, rows = other_ref.shape
    width = out_refs[0].shape[2]
    each = rows // width
    for tile in range(tiles):
        mixed, total, top = combined([own_ref[tile], other_ref[tile]])
        for i in range(each):
            out = out_refs[tile * each + i]
            cut = slice(i * width, (i + 1) * width)
            rows_out = [mixed[:, cut]] + spread(total[:, cut]) + spread(top[:, cut])
            out[0] = jnp.concatenate(rows_out, axis=0).astype(jnp.bfloat16)


def fold(own, other, width):
    tiles, _, rows = other.shape
    return pl.pallas_call(
        fold_kernel,
        name="fold",
        out_shape=[jax.ShapeDtypeStruct((1, ROWS, width), jnp.bfloat16)] * (tiles * rows // width),
        cost_estimate=pl.CostEstimate(flops=1024, bytes_accessed=1024, transcendentals=0),
        compiler_params=pltpu.CompilerParams(vmem_limit_bytes=12 * 2**20),
    )(own, other)


def outgoing_kernel(*refs):
    *sources, out_ref, held, chunks, semaphores, leave = refs
    count = len(sources)
    token_rows = sources[0].shape[0]
    piece = token_rows // 4
    at = count * token_rows
    depth = token_rows // 3

    def arriving(i):
        cuts = [pl.ds(j * depth, depth) for j in range(3)]
        return [
            pltpu.make_async_copy(sources[i].at[cut], held.at[i, cut], semaphores.at[i, j]) for j, cut in enumerate(cuts)
        ]

    for i in range(count):
        for copy in arriving(i):
            copy.start()
    for i in range(count):
        for copy in arriving(i):
            copy.wait()
    leaving = []
    for target in range(16):
        z, yh, yl = target // 4, target // 2 % 2, target % 2
        head = 10 * yl + 2 * z + yh
        for i in range(count):
            chunks[target, i * token_rows : (i + 1) * token_rows, :] = held[i, :, head * HS : (head + 1) * HS]
        head = 10 * yl + 8 + yh
        pieces = [
            held[i, :, head * HS : (head + 1) * HS].astype(jnp.float32)[z * piece : (z + 1) * piece] for i in range(count)
        ]
        pieces.append(jnp.zeros((chunks.shape[1] - at - count * piece, HS), jnp.float32))
        chunks[target, at:, :] = jnp.concatenate(pieces, axis=0).astype(jnp.bfloat16)
        leaving.append(pltpu.make_async_copy(chunks.at[target], out_ref.at[target], leave.at[target]))
        leaving[-1].start()
    for copy in leaving:
        copy.wait()


def outgoing(name, *arrays):
    rows = len(arrays) * arrays[0].shape[0] * 5 // 4
    rows += -rows % 16
    return pl.pallas_call(
        outgoing_kernel,
        name=name,
        in_specs=[pl.BlockSpec(memory_space=pl.ANY)] * len(arrays),
        out_specs=pl.BlockSpec(memory_space=pl.ANY),
        out_shape=jax.ShapeDtypeStruct((16, rows, HS), jnp.bfloat16),
        scratch_shapes=[
            pltpu.VMEM((len(arrays), *arrays[0].shape), jnp.bfloat16),
            pltpu.VMEM((16, rows, HS), jnp.bfloat16),
            pltpu.SemaphoreType.DMA((len(arrays), 3)),
            pltpu.SemaphoreType.DMA((16,)),
        ],
        cost_estimate=pl.CostEstimate(flops=1024, bytes_accessed=1024, transcendentals=0),
        compiler_params=pltpu.CompilerParams(vmem_limit_bytes=60 * 2**20),
    )(*arrays)


def project_kernel(core_ref, att_ref, own_w, side_w, kept_ref, above_ref, below_ref, held, semaphores, *, start):
    core = core_ref[0]
    kept, half = kept_ref.shape[0], above_ref.shape[0]
    steps = kept_ref.shape[1] // WIDTH

    def columns(j, base=0):
        return pl.ds(pl.multiple_of(base + j * WIDTH, HS), WIDTH)

    def arriving(j):
        return pltpu.make_async_copy(side_w.at[:, columns(j, start)], held.at[j], semaphores.at[j])

    for j in range(steps):
        arriving(j).start()

    def group(number):
        return jnp.concatenate([att_ref[number * 5 + i] for i in range(5)], axis=1)

    own, side = group(core), group(1 - core)

    @pl.loop(0, steps)
    def _(j):
        total = jnp.dot(own, own_w[:, columns(j, start)], preferred_element_type=jnp.float32)
        arriving(j).wait()
        total = total + jnp.dot(side, held[j], preferred_element_type=jnp.float32)
        kept_ref[:, columns(j)] = total[:kept].astype(jnp.bfloat16)
        above_ref[:, columns(j)] = total[kept : kept + half].astype(jnp.bfloat16)
        below_ref[:, columns(j)] = total[kept + half :].astype(jnp.bfloat16)


def project(core, attended, own_w, side_w, start, columns):
    rows, steps = attended.shape[1], columns // WIDTH
    return pl.pallas_call(
        functools.partial(project_kernel, start=start),
        name="project",
        in_specs=[
            pl.BlockSpec(memory_space=pltpu.SMEM),
            pl.BlockSpec(memory_space=pltpu.VMEM),
            pl.BlockSpec(memory_space=pltpu.VMEM),
            pl.BlockSpec(memory_space=pl.ANY),
        ],
        out_shape=[
            jax.ShapeDtypeStruct((rows // 2, columns), jnp.bfloat16),
            jax.ShapeDtypeStruct((rows // 4, columns), jnp.bfloat16),
            jax.ShapeDtypeStruct((rows // 4, columns), jnp.bfloat16),
        ],
        scratch_shapes=[
            pltpu.VMEM((steps, side_w.shape[0], WIDTH), jnp.bfloat16),
            pltpu.SemaphoreType.DMA((steps,)),
        ],
        cost_estimate=pl.CostEstimate(flops=1024, bytes_accessed=1024, transcendentals=0),
        compiler_params=pltpu.CompilerParams(vmem_limit_bytes=24 * 2**20),
    )(core, attended, own_w, side_w)


def ring(array, axes, size, shift, name="ring"):
    with jax.named_scope(name):
        return lax.ppermute(array, axes, [(i, (i + shift) % size) for i in range(size)])


def cross(array, axis, bit, name):
    with jax.named_scope(name):
        return lax.ppermute(array, axis, [(i, i ^ bit) for i in range(4)])


def swap(array, name="swap"):
    with jax.named_scope(name):
        return lax.ppermute(array, "c", [(0, 1), (1, 0)])


def mask_tables(block_mask, frame_map):
    x, z, core = lax.axis_index("x"), lax.axis_index("z"), lax.axis_index("c")
    low, group = np.arange(2)[None, :, None], np.arange(3)
    at_core = np.arange(2)[:, None, None]
    ring_within = ((low * 2 + at_core) * 96 + group * 32) // BLOCK
    at_z = np.arange(4)[:, None, None, None]
    plane_within = ((low * 2 + at_core) * 96 + at_z * 24 + group * 8) // BLOCK

    def frames(at_x):
        return lax.dynamic_slice_in_dim(frame_map, at_x * 8, 8)[:, None, None] * FB

    def ring_blocks(at_x, at_core):
        within = jnp.asarray(ring_within.astype(np.int32))[at_core]
        return (frames(at_x) + within[None]).reshape(-1)

    def plane_blocks(at_x, at_core, at_z):
        within = jnp.asarray(plane_within.astype(np.int32))[at_z, at_core]
        return (frames(at_x) + within[None]).reshape(-1)

    ring_keys = jnp.concatenate([ring_blocks((x + i) % 4, core) for i in NEAR])
    plane_keys = jnp.concatenate([plane_blocks(x, core, z ^ i) for i in (0, 2, 3, 1)])
    blocks = jnp.arange(block_mask.shape[0], dtype=jnp.int32)
    pad = jnp.zeros((32,), jnp.int32)
    ring_queries, plane_queries = [], []
    for side in (0, 1):
        ring_queries += [ring_blocks(x, core ^ side), pad, pad, pad[:16]]
        for pair in (0, 2):
            plane_queries += [plane_blocks(x ^ (pair + i), core ^ side, z) for i in (0, 1)] + [pad]
    blocked = (block_mask <= 0).astype(jnp.bfloat16)

    def pick(index):
        return (index[:, None] == blocks[None, :]).astype(jnp.bfloat16)

    queries = pick(jnp.concatenate(ring_queries + plane_queries))
    by_query = jnp.dot(queries, blocked, preferred_element_type=jnp.float32).astype(jnp.bfloat16).reshape(6, HS, -1)

    def table(index, part):
        found = jnp.einsum("kb,tcb->tkc", pick(index), part, preferred_element_type=jnp.float32)
        return found * NEG

    return table(ring_keys, by_query[:2]), table(plane_keys, by_query[2:])


def local(queries, keys, values, w_out, block_mask, frame_map):
    core = lax.axis_index("c").astype(jnp.int32)
    z, low = lax.axis_index("z"), lax.axis_index("yl")
    token_rows = queries.shape[0]
    piece = token_rows // 4

    side_w = swap(w_out, "side_w")
    with jax.named_scope("spread"):
        sent = lax.all_to_all(outgoing("outgoing", keys, values, queries), RING, 0, 0)
    one, two, three = token_rows, 2 * token_rows, 3 * token_rows
    ring_kv = jnp.concatenate([sent[:, :one], sent[:, one:two]], axis=0).reshape(-1, HS)
    ring_q = sent[:, two:three].reshape(-1, HS)
    plane_kv = jnp.concatenate([sent[:, three : three + piece], sent[:, three + piece : three + 2 * piece]], axis=0)
    plane_kv = plane_kv.reshape(-1, HS)
    plane_q = sent[:, three + 2 * piece : three + 3 * piece].reshape(-1, HS)
    ring_rows = 16 * token_rows
    plane_rows = 16 * piece

    ring_masks, plane_masks = mask_tables(block_mask, frame_map)

    side_w, ring_kv, ring_q, plane_kv, plane_q = lax.optimization_barrier((side_w, ring_kv, ring_q, plane_kv, plane_q))
    ring_left, ring_right = ring(ring_kv, "x", 4, 1, "ring_x"), ring(ring_kv, "x", 4, -1, "ring_x")
    query_a = jnp.stack([ring_q, swap(ring_q, "swap_q")])

    plane_kv = [plane_kv] + [cross(plane_kv, "z", i, "plane_z") for i in (2, 3, 1)]
    plane_q = jnp.concatenate([plane_q] + [cross(plane_q, "x", i, "plane_q") for i in (1, 2, 3)], axis=0)
    query_b = jnp.concatenate([plane_q, swap(plane_q, "swap_plane_q")], axis=0).reshape(4, 2 * plane_rows, HS)
    query_a, query_b = lax.optimization_barrier((query_a, query_b))
    whole = [(0, 0, 0, ring_rows, ring_rows)]
    state = attention("own", query_a, ring_masks[:, :48], 32, [ring_kv], whole)
    plane_parts = [(i, 0, i, plane_rows, plane_rows) for i in range(4)]
    query_b, state = lax.optimization_barrier((query_b, state))
    plane_state = attention("plane", query_b, plane_masks, 8, plane_kv, plane_parts, small=128)

    plane_state, state, ring_left, ring_right = lax.optimization_barrier((plane_state, state, ring_left, ring_right))
    other_b = swap(plane_state[0][2:], "swap_b")
    middle = ring_kv.shape[0] // 2
    ring_far = [
        ring(ring_left[:middle], "x", 4, 1, "ring_x_far"),
        ring(ring_right[middle:], "x", 4, -1, "ring_x_far"),
    ]
    plane_part = fold(plane_state[0], other_b, plane_rows)
    plane_part, state = lax.optimization_barrier((plane_part, state))
    plane_part = [plane_part[0]] + [cross(plane_part[i], "x", i, "plane_sum") for i in (1, 2, 3)]
    state = attention("left", query_a, ring_masks[:, 48:96], 32, [ring_left], whole, state)
    state = attention("right", query_a, ring_masks[:, 96:144], 32, [ring_right], whole, state)
    out_b = merge("merge_plane", *plane_part).reshape(4, 2, 2, piece, HS)
    out_b, state = lax.optimization_barrier((out_b, state))
    far = [(0, 0, 1, 0, ring_rows)]
    far_masks = ring_masks[:, 144:]
    side = attention("far_side", query_a, far_masks, 32, ring_far, far, state, skip=1, tiles=1)
    other_a = swap(side[0], "swap_a")
    state, side = lax.optimization_barrier((state, side))
    own = attention("far_own", query_a, far_masks, 32, ring_far, far, state, skip=0, tiles=1)
    out_a = merge("merge_ring", own[0], other_a, cost=1 << 32).reshape(4, 2, 2, token_rows, HS)

    def split(array):
        first, second = array[:, :, 0], array[:, :, 1]
        same = jnp.where(low == 0, first, second)
        other = jnp.where(low == 0, second, first)
        flipped = jnp.stack([other[:, 1], other[:, 0]], axis=1)
        below = jnp.where(low == 0, flipped, other)
        above = jnp.where(low == 0, other, flipped)
        return same, below, above

    half = token_rows // 2
    same, below, above = split(out_a)
    piece_same, piece_below, piece_above = split(out_b)
    back = jnp.concatenate(
        [same, below[:, :, :half], above[:, :, half:], piece_same, jnp.where(z < 2, piece_below, piece_above)], axis=2
    ).reshape(8, -1, HS)
    with jax.named_scope("return"):
        back = lax.all_to_all(back, ("z", "yh"), 0, 0)
    rows = 2 * token_rows
    plane_back = back[:, rows:].reshape(4, 2, 2, piece, HS).transpose(1, 2, 0, 3, 4).reshape(2, rows, HS)
    attended = jnp.concatenate([back[:, :rows], plane_back], axis=0)

    outs = []
    columns = w_out.shape[1] // CHUNKS
    for i in range(CHUNKS):
        kept, to_below, to_above = project(core[None], attended, w_out, side_w, i * columns, columns)
        from_above, from_below = ring(to_below, Y, 4, -1, "sum_y"), ring(to_above, Y, 4, 1, "sum_y")
        other = jnp.concatenate([from_above, from_below], axis=0)
        out = (kept.astype(jnp.float32) + other.astype(jnp.float32)).astype(jnp.bfloat16)
        outs.append(out if i == CHUNKS - 1 else lax.optimization_barrier(out))
    return outs[0] if CHUNKS == 1 else jnp.concatenate(outs, axis=1)


def solution(mesh):
    fine = jax.sharding.Mesh(mesh.devices.reshape(4, 4, 2, 2, 2), ALL)
    rows = P(ALL, None)
    placed = (rows, rows, rows, P(("yl", "c"), None), P(), P())
    return jax.shard_map(local, mesh=fine, in_specs=placed, out_specs=rows, check_vma=False)
```
